256 devices in a mesh: rep: 2 (over y_lo), seq: 64 (over x, z, core), chan: 2 (over y_hi).
Axes of the slice: x: 4, y: 4 (y_hi: 2, y_lo: 2; y = y_hi * 2 + y_lo), z: 8, core: 2. Of those that a mesh axis runs over, the one named last changes fastest.
Arguments:
- inputs: bfloat16 [2, 65536, 256], P('rep', 'seq', 'chan'), may hold values from -6 to 6
- cotangent: bfloat16 [2, 65536, 256], P('rep', 'seq', 'chan'), may hold values from -0.015625 to 0.015625
- filter_taps: bfloat16 [65536, 256], P('seq', 'chan'), may hold values from -6 to 6
- out_proj: bfloat16 [256, 256], P('chan'), may hold values from -0.375 to 0.375
Outputs:
- grad_input: bfloat16 [2, 65536, 256], P('rep', 'seq', 'chan')
- grad_filter: float32 [65536, 256], P('seq', 'chan')
The draws below stay inside these ranges and needn't reach their ends.
All inputs are finite; a program needn't handle non-finite values.
Results may differ from the reference program's by a relative error of at most 0.0049.
Values may be sent and summed in bfloat16 or wider, within the bound.
A program may use at most 128 MiB of HBM per device.

```python
import jax
import jax.numpy as jnp

C = 256
LENGTH = 65536
SEQS = 2


def level_of(key, shape, split, smallest, largest):
    level = 1.0
    for axis_at, parts in split:
        steps = jax.random.uniform(jax.random.fold_in(jax.random.fold_in(key, 6), axis_at), (parts,), jnp.float32, smallest / len(split), largest / len(split))
        level = level * jnp.repeat(jnp.exp(steps), shape[axis_at] // parts).reshape((-1,) + (1,) * (len(shape) - 1 - axis_at))
    return level


def bell_draw(stream_key, shape, deviation, limit, cuts=(), held_as=jnp.bfloat16):
    entries = jax.random.normal(stream_key, shape, jnp.float32) * deviation
    if len(cuts) > 0:
        entries = level_of(stream_key, shape, cuts, -0.22, 0.18) * entries
    return jnp.clip(entries, min=-limit, max=limit).astype(held_as)


def setup_inputs(seed: int = 0) -> dict:
    keys = jax.random.split(jax.random.key(seed), 5)
    return {
        "inputs": bell_draw(keys[0], (SEQS, LENGTH, C), 1.0, 6.0, ((0, 2), (1, 64), (2, 2))),
        "cotangent": bell_draw(keys[1], (SEQS, LENGTH, C), ((2 * LENGTH) ** -0.5), 0.015625, ((0, 2), (1, 64), (2, 2))),
        "filter_taps": bell_draw(keys[2], (LENGTH, C), 1.0, 6.0, ((0, 64), (1, 2))),
        "out_proj": bell_draw(keys[3], (C, C), C ** -0.5, 0.375, ((0, 2),)),
    }


def reference(inputs, cotangent, filter_taps, out_proj):
    extent = 2 * LENGTH
    grad_mixed = jnp.dot(cotangent.reshape(SEQS * LENGTH, C), out_proj.T, preferred_element_type=jnp.float32)
    grad_mixed = grad_mixed.astype(jnp.bfloat16).reshape(SEQS, LENGTH, C)
    width_block = min(256, C)
    input_cols = []
    filter_cols = []
    for col_start in range(0, C, width_block):
        col_end = col_start + width_block
        filter_spec = jnp.fft.fft(filter_taps[:, col_start:col_end].astype(jnp.float32), n=extent, axis=0)
        grad_list = []
        spec_sum = None
        for member in range(SEQS):
            grad_spec = jnp.fft.fft(grad_mixed[member, :, col_start:col_end].astype(jnp.float32), n=extent, axis=0)
            input_spec = jnp.fft.fft(inputs[member, :, col_start:col_end].astype(jnp.float32), n=extent, axis=0)
            grad_list.append(jnp.fft.ifft(grad_spec * jnp.conj(filter_spec), axis=0)[:LENGTH].real.astype(jnp.bfloat16))
            spec_term = grad_spec * jnp.conj(input_spec)
            spec_sum = spec_term if spec_sum is None else spec_sum + spec_term
        input_cols.append(jnp.stack(grad_list))
        filter_cols.append(jnp.fft.ifft(spec_sum, axis=0)[:LENGTH].real.astype(jnp.float32))
    return jnp.concatenate(input_cols, axis=2), jnp.concatenate(filter_cols, axis=1)
```

```python
import math

import jax
import jax.numpy as jnp
import numpy as np
from jax import lax
from jax.sharding import PartitionSpec as P

precise_mode = lax.Precision.HIGHEST
LANES = 128


def tables(length):
    rows = length // LANES
    row_index = np.arange(rows)
    lane_index = np.arange(LANES)
    row_angle = ((4 * row_index[:, None] + 1) * row_index[None, :] % (4 * rows)) * (2.0 * math.pi / (4 * rows))
    twist_angle = ((4 * row_index[:, None] + 1) * lane_index[None, :] % (4 * length)) * (2.0 * math.pi / (4 * length))
    lane_angle = (lane_index[:, None] * lane_index[None, :] % LANES) * (2.0 * math.pi / LANES)
    row_forward = np.concatenate([np.cos(row_angle), -np.sin(row_angle)], axis=0)
    row_inverse = np.concatenate([np.cos(row_angle).T, -np.sin(row_angle).T], axis=1) / length
    lane_cos, lane_sin = np.cos(lane_angle), np.sin(lane_angle)
    lane_forward = np.block([[lane_cos, -lane_sin], [lane_sin, lane_cos]])
    lane_inverse = np.block([[lane_cos, lane_sin], [-lane_sin, lane_cos]])
    return [
        np.asarray(table, np.float32)
        for table in (row_forward, row_inverse, lane_forward, lane_inverse, np.cos(twist_angle), np.sin(twist_angle))
    ]


def product(left, right):
    return jnp.dot(left, right, precision=precise_mode, preferred_element_type=jnp.float32)


def correlate(grads, signals, taps):
    length = taps.shape[0]
    rows = length // LANES
    row_forward, row_inverse, lane_forward, lane_inverse, twist_cos, twist_sin = tables(length)
    stacked = jnp.concatenate([grads, signals, taps[None]], axis=0).astype(jnp.float32)
    count = stacked.shape[0]
    stacked = stacked.reshape(count, rows, LANES).transpose(1, 0, 2).reshape(rows, count * LANES)
    outer = product(row_forward, stacked).reshape(2, rows, count, LANES)
    cosine, sine = twist_cos[:, None, :], twist_sin[:, None, :]
    twisted = jnp.concatenate(
        [outer[0] * cosine + outer[1] * sine, outer[1] * cosine - outer[0] * sine], axis=-1
    )
    spectra = product(twisted.transpose(1, 0, 2).reshape(count * rows, 2 * LANES), lane_forward)
    spectra = spectra.reshape(count, rows, 2, LANES)
    real, imag = spectra[:, :, 0], spectra[:, :, 1]

    def conj_product(first, second):
        return jnp.concatenate(
            [
                real[first] * real[second] + imag[first] * imag[second],
                imag[first] * real[second] - real[first] * imag[second],
            ],
            axis=-1,
        )

    joined = jnp.concatenate(
        [conj_product(0, 4), conj_product(1, 4), conj_product(0, 2) + conj_product(1, 3)], axis=0
    )
    inner = product(joined, lane_inverse).reshape(3, rows, 2, LANES)
    real, imag = inner[:, :, 0], inner[:, :, 1]
    untwisted = jnp.stack(
        [real * twist_cos - imag * twist_sin, imag * twist_cos + real * twist_sin]
    )
    untwisted = untwisted.transpose(0, 2, 1, 3).reshape(2 * rows, 3 * LANES)
    result = product(row_inverse, untwisted)
    return result.reshape(rows, 3, LANES).transpose(1, 0, 2).reshape(3, length)


def per_device(inputs, cotangent, filter_taps, out_proj):
    devices = lax.axis_size("seq")
    members = lax.axis_size("rep")
    member = lax.axis_index("rep")
    tok_rows, chan_width = filter_taps.shape
    gathered = lax.all_gather(cotangent.reshape(tok_rows, chan_width), "chan", axis=1, tiled=True)
    grad_mixed = lax.dot_general(
        out_proj, gathered, (((1,), (1,)), ((), ())), preferred_element_type=jnp.float32
    ).astype(jnp.bfloat16)
    signal = inputs.reshape(tok_rows, chan_width).T
    half = tok_rows // members
    taps = lax.dynamic_slice_in_dim(filter_taps, member * half, half, axis=0).T
    outgoing = jnp.concatenate([grad_mixed, signal, taps], axis=1)
    arrived = lax.all_to_all(outgoing, ("rep", "seq"), split_axis=0, concat_axis=0, tiled=True)
    arrived = arrived.reshape(members, devices, 2 * tok_rows + half)
    grads = arrived[:, :, :tok_rows].reshape(members, devices * tok_rows)
    signals = arrived[:, :, tok_rows : 2 * tok_rows].reshape(members, devices * tok_rows)
    taps = arrived[:, :, 2 * tok_rows :].transpose(1, 0, 2).reshape(devices * tok_rows)
    result = correlate(grads, signals, taps).astype(jnp.bfloat16)
    result = result.reshape(3, devices, tok_rows)
    outgoing = jnp.stack([result[:2], jnp.broadcast_to(result[2:], (2, devices, tok_rows))], axis=2)
    outgoing = outgoing.reshape(members * devices, 2 * tok_rows)
    arrived = lax.all_to_all(outgoing, ("rep", "seq"), split_axis=0, concat_axis=0, tiled=True)
    grad_input = arrived[:, :tok_rows].T
    grad_filter = arrived[:, tok_rows:].T.astype(jnp.float32)
    return (grad_input.reshape(1, tok_rows, chan_width), grad_filter)


def solution(mesh):
    return jax.shard_map(
        per_device,
        mesh=mesh,
        in_specs=(
            P("rep", "seq", "chan"),
            P("rep", "seq", "chan"),
            P("seq", "chan"),
            P("chan", None),
        ),
        out_specs=(P("rep", "seq", "chan"), P("seq", "chan")),
        check_vma=False,
    )
```

```python
import functools
import math

import jax
import jax.numpy as jnp
import numpy as np
from jax import lax
from jax.experimental import pallas as pl
from jax.experimental.pallas import tpu as pltpu
from jax.sharding import PartitionSpec as P

LANES = 128
SUB = 8
MESH = pl.DeviceIdType.MESH
COT, SIG, TAP, GRAD, FILT, INP = range(6)
KINDS = 6


def split_high_low(table):
    high = np.asarray(table, np.float32).astype(jnp.bfloat16)
    low = (table - high.astype(np.float64)).astype(np.float32).astype(jnp.bfloat16)
    return np.stack([high, low])


def tables(length):
    rows = length // LANES
    row_index = np.arange(rows)
    lane_index = np.arange(LANES)
    row_angle = ((4 * row_index[:, None] + 1) * row_index[None, :] % (4 * rows)) * (2.0 * math.pi / (4 * rows))
    twist_angle = ((4 * row_index[:, None] + 1) * lane_index[None, :] % (4 * length)) * (2.0 * math.pi / (4 * length))
    lane_angle = (lane_index[:, None] * lane_index[None, :] % LANES) * (2.0 * math.pi / LANES)
    row_forward = np.concatenate([np.cos(row_angle), -np.sin(row_angle)], axis=0)
    lane_cos, lane_sin = np.cos(lane_angle), np.sin(lane_angle)
    lane_forward = np.block([[lane_cos, -lane_sin], [lane_sin, lane_cos]])
    lane_inverse = np.block([[lane_cos, lane_sin], [-lane_sin, lane_cos]])
    return (
        split_high_low(row_forward),
        split_high_low(row_forward.T / length),
        np.concatenate([split_high_low(lane_forward), split_high_low(lane_inverse)], axis=0),
        np.stack([np.cos(twist_angle), np.sin(twist_angle)]).astype(np.float32),
    )


def dot(left, right):
    return jnp.dot(left, right, preferred_element_type=jnp.float32)


def dot_three(left, high, low):
    left_high = left.astype(jnp.bfloat16)
    left_low = (left - left_high.astype(jnp.float32)).astype(jnp.bfloat16)
    return dot(left_high, high) + (dot(left_low, high) + dot(left_high, low))


def kernel(
    members, devices,
    signal_ref, cot_ref, taps_ref, proj_ref, forward_hbm, inverse_hbm, lane_hbm, twist_hbm,
    input_out, filter_out,
    forward, inverse, lane, twist, work, cots,
    signal_send, taps_send, grad_send, filter_send, input_send,
    signal_got, taps_got, grad_got, filter_got, input_got,
    spectra, send_sem, recv_sem, table_sem,
):
    member = lax.axis_index("rep")
    place = lax.axis_index("seq")
    half = lax.axis_index("chan")
    owners = members * devices
    me = member * devices + place
    rows = devices * SUB
    width = signal_ref.shape[1]
    chunk = signal_ref.shape[0] // SUB

    barrier = pltpu.get_barrier_semaphore()

    def target(step):
        other = lax.rem(me + step, owners)
        return other, {"rep": other // devices, "seq": lax.rem(other, devices)}

    def greet(step, carry):
        pl.semaphore_signal(barrier, inc=1, device_id=target(step)[1], device_id_type=MESH)
        return carry

    lax.fori_loop(1, owners, greet, 0)
    partner = {"chan": 1 - half}
    pl.semaphore_signal(barrier, inc=1, device_id=partner, device_id_type=MESH)

    table_copies = [
        pltpu.make_async_copy(source, target_ref, table_sem.at[at])
        for at, (source, target_ref) in enumerate(
            ((forward_hbm, forward), (lane_hbm, lane), (twist_hbm, twist), (inverse_hbm, inverse))
        )
    ]
    for copy in table_copies:
        copy.start()

    def spread(source, target_ref):
        for j in range(SUB):
            work[pl.ds(j, width, stride=SUB), :] = source(j)
        target_ref[...] = work[...].reshape(width, SUB, LANES).astype(jnp.bfloat16)

    def block_of(ref):
        return lambda j: ref[j * chunk : (j + 1) * chunk, :].astype(jnp.float32).T

    spread(block_of(taps_ref), taps_send)
    spread(block_of(signal_ref), signal_send)
    pl.semaphore_wait(barrier, owners)

    cot_copy = pltpu.make_async_remote_copy(
        src_ref=cot_ref, dst_ref=cots.at[half], send_sem=send_sem.at[COT], recv_sem=recv_sem.at[COT],
        device_id=partner, device_id_type=MESH,
    )
    cot_copy.start()

    def exchange(kind, send_ref, got_ref):
        def send(step, carry):
            other, place_of = target(step)
            pltpu.make_async_remote_copy(
                src_ref=send_ref.at[other], dst_ref=got_ref.at[me],
                send_sem=send_sem.at[kind], recv_sem=recv_sem.at[kind],
                device_id=place_of, device_id_type=MESH,
            ).start()
            return carry

        lax.fori_loop(1, owners, send, 0)
        pltpu.make_async_copy(send_ref.at[me], got_ref.at[me], recv_sem.at[kind]).start()

    def arrived(kind, got_ref):
        pltpu.make_async_copy(got_ref, got_ref, recv_sem.at[kind]).wait()

    def sent(kind, send_ref, count):
        part = send_ref.at[pl.ds(0, count)]
        pltpu.make_async_copy(part, part, send_sem.at[kind]).wait()

    def send_taps(step, carry):
        other = lax.rem(place + step, devices)
        pltpu.make_async_remote_copy(
            src_ref=taps_send.at[member * devices + other], dst_ref=taps_got.at[place],
            send_sem=send_sem.at[TAP], recv_sem=recv_sem.at[TAP],
            device_id={"seq": other}, device_id_type=MESH,
        ).start()
        return carry

    lax.fori_loop(1, devices, send_taps, 0)
    pltpu.make_async_copy(taps_send.at[me], taps_got.at[place], recv_sem.at[TAP]).start()
    exchange(SIG, signal_send, signal_got)

    cots[half] = cot_ref[...]
    cot_copy.wait()

    def mixed(j):
        total = None
        for part in range(2):
            term = lax.dot_general(
                proj_ref[:, part * width : (part + 1) * width],
                cots[part, j * chunk : (j + 1) * chunk, :],
                (((1,), (1,)), ((), ())),
                preferred_element_type=jnp.float32,
            )
            total = term if total is None else total + term
        return total

    spread(mixed, grad_send)
    exchange(GRAD, grad_send, grad_got)

    for copy in table_copies:
        copy.wait()

    def transform(values, first):
        outer = dot(forward[0], values) + dot(forward[1], values)
        for at in range(values.shape[1] // LANES):
            real = outer[:rows, at * LANES : (at + 1) * LANES]
            imag = outer[rows:, at * LANES : (at + 1) * LANES]
            twisted = jnp.concatenate(
                [real * twist[0] + imag * twist[1], imag * twist[0] - real * twist[1]], axis=1
            )
            spectra[first + at] = dot_three(twisted, lane[0], lane[1])

    def member_rows(ref, at):
        return ref[at * devices : (at + 1) * devices].reshape(rows, LANES)

    def gathered(ref):
        return jnp.concatenate([member_rows(ref, at) for at in range(members)], axis=1)

    arrived(TAP, taps_got)
    arrived(SIG, signal_got)
    transform(jnp.concatenate([gathered(signal_got), taps_got[...].reshape(rows, LANES)], axis=1), 0)
    arrived(GRAD, grad_got)
    transform(gathered(grad_got), 3)

    def conj_product(first, second):
        first_real, first_imag = spectra[first, :, :LANES], spectra[first, :, LANES:]
        second_real, second_imag = spectra[second, :, :LANES], spectra[second, :, LANES:]
        return (
            first_real * second_real + first_imag * second_imag,
            first_imag * second_real - first_real * second_imag,
        )

    def untransform(pair):
        inner = dot_three(jnp.concatenate(pair, axis=1), lane[2], lane[3])
        real, imag = inner[:, :LANES], inner[:, LANES:]
        return jnp.concatenate(
            [real * twist[0] - imag * twist[1], imag * twist[0] + real * twist[1]], axis=0
        )

    def rows_inverse(values):
        high = values.astype(jnp.bfloat16)
        low = (values - high.astype(jnp.float32)).astype(jnp.bfloat16)
        return dot(inverse[0], high) + (dot(inverse[0], low) + dot(inverse[1], high))

    filter_terms = [conj_product(3 + at, at) for at in range(2)]
    filter_pair = tuple(first + second for first, second in zip(*filter_terms))
    filter_rows = rows_inverse(untransform(filter_pair)).astype(jnp.bfloat16).reshape(devices, SUB, LANES)
    for at in range(members):
        filter_send[at * devices : (at + 1) * devices] = filter_rows
    exchange(FILT, filter_send, filter_got)

    input_rows = rows_inverse(
        jnp.concatenate([untransform(conj_product(3 + at, 2)) for at in range(2)], axis=1)
    ).astype(jnp.bfloat16)
    for at in range(members):
        input_send[at * devices : (at + 1) * devices] = input_rows[
            :, at * LANES : (at + 1) * LANES
        ].reshape(devices, SUB, LANES)
    exchange(INP, input_send, input_got)

    def collect(got_ref, out_ref):
        work[...] = got_ref[...].astype(jnp.float32).reshape(width * SUB, LANES)
        for j in range(SUB):
            out_ref[j * chunk : (j + 1) * chunk, :] = work[pl.ds(j, width, stride=SUB), :].T.astype(
                out_ref.dtype
            )

    sent(TAP, taps_send, devices - 1)
    sent(SIG, signal_send, owners - 1)
    sent(GRAD, grad_send, owners - 1)
    arrived(FILT, filter_got)
    collect(filter_got, filter_out)
    arrived(INP, input_got)
    collect(input_got, input_out)
    sent(FILT, filter_send, owners - 1)
    sent(INP, input_send, owners - 1)


def per_device(inputs, cotangent, filter_taps, out_proj):
    devices = lax.axis_size("seq")
    members = lax.axis_size("rep")
    tok_rows, width = filter_taps.shape
    owners = members * devices
    rows = devices * SUB
    constants = [jnp.asarray(table) for table in tables(devices * tok_rows)]
    vmem = pl.BlockSpec(memory_space=pltpu.VMEM)
    hbm = pl.BlockSpec(memory_space=pl.ANY)
    message = (owners, SUB, LANES)
    grad_input, grad_filter = pl.pallas_call(
        functools.partial(kernel, members, devices),
        out_shape=(
            jax.ShapeDtypeStruct((tok_rows, width), jnp.bfloat16),
            jax.ShapeDtypeStruct((tok_rows, width), jnp.float32),
        ),
        in_specs=[vmem] * 4 + [hbm] * 4,
        out_specs=(vmem, vmem),
        scratch_shapes=[pltpu.VMEM(table.shape, table.dtype) for table in constants]
        + [
            pltpu.VMEM((width * SUB, LANES), jnp.float32),
            pltpu.VMEM((2, tok_rows, width), jnp.bfloat16),
        ]
        + [pltpu.VMEM(message, jnp.bfloat16)] * 5
        + [
            pltpu.VMEM(message, jnp.bfloat16),
            pltpu.VMEM((devices, SUB, LANES), jnp.bfloat16),
            pltpu.VMEM(message, jnp.bfloat16),
            pltpu.VMEM(message, jnp.bfloat16),
            pltpu.VMEM(message, jnp.bfloat16),
            pltpu.VMEM((5, rows, 2 * LANES), jnp.float32),
            pltpu.SemaphoreType.DMA((KINDS,)),
            pltpu.SemaphoreType.DMA((KINDS,)),
            pltpu.SemaphoreType.DMA((4,)),
        ],
        compiler_params=pltpu.CompilerParams(
            collective_id=0, has_side_effects=True, vmem_limit_bytes=48 * 1024 * 1024
        ),
        name="correlate",
    )(
        inputs.reshape(tok_rows, width),
        cotangent.reshape(tok_rows, width),
        filter_taps,
        out_proj,
        *constants,
    )
    return (grad_input.reshape(1, tok_rows, width), grad_filter)


def solution(mesh):
    return jax.shard_map(
        per_device,
        mesh=mesh,
        in_specs=(
            P("rep", "seq", "chan"),
            P("rep", "seq", "chan"),
            P("seq", "chan"),
            P("chan", None),
        ),
        out_specs=(P("rep", "seq", "chan"), P("seq", "chan")),
        check_vma=False,
    )
```

```python
import functools
import math

import jax
import jax.numpy as jnp
import numpy as np
from jax import lax
from jax.experimental import pallas as pl
from jax.experimental.pallas import tpu as pltpu
from jax.sharding import PartitionSpec as P

LANES = 128
SUB = 8
STEP = 128
WAVES = 8
VMEM_LIMIT = 60 * 1024 * 1024
MESH = pl.DeviceIdType.MESH
COT, SIG, TAP, GRAD, FILT, INP, SWAP = range(7)
KINDS = 7


def split_high_low(table):
    high = np.asarray(table, np.float32).astype(jnp.bfloat16)
    low = (table - high.astype(np.float64)).astype(np.float32).astype(jnp.bfloat16)
    return np.stack([high, low])


def tables(length):
    rows = length // LANES
    row_index = np.arange(rows)
    lane_index = np.arange(LANES)
    row_angle = ((4 * row_index[:, None] + 1) * row_index[None, :] % (4 * rows)) * (2.0 * math.pi / (4 * rows))
    twist_angle = ((4 * row_index[:, None] + 1) * lane_index[None, :] % (4 * length)) * (2.0 * math.pi / (4 * length))
    lane_angle = (lane_index[:, None] * lane_index[None, :] % LANES) * (2.0 * math.pi / LANES)
    row_forward = np.concatenate([np.cos(row_angle), -np.sin(row_angle)], axis=0)
    lane_cos, lane_sin = np.cos(lane_angle), np.sin(lane_angle)
    lane_forward = np.block([[lane_cos, -lane_sin], [lane_sin, lane_cos]])
    lane_inverse = np.block([[lane_cos, lane_sin], [-lane_sin, lane_cos]])
    forward_high, forward_low = split_high_low(row_forward)
    lane_tables = []
    for table in (lane_forward, lane_inverse):
        high, low = split_high_low(table)
        lane_tables.append(np.concatenate([high, high, low], axis=0))
    return (
        np.concatenate([forward_high, forward_low], axis=1),
        split_high_low(row_forward.T / length),
        np.stack(lane_tables),
        np.stack([np.cos(twist_angle), np.sin(twist_angle)]).astype(np.float32),
    )


def dot(left, right):
    return jnp.dot(left, right, preferred_element_type=jnp.float32)


def transposed(block):
    at_row = lax.broadcasted_iota(jnp.int32, block.shape, 0)
    at_lane = lax.broadcasted_iota(jnp.int32, block.shape, 1)
    identity = jnp.where(at_row == at_lane, 1.0, 0.0).astype(jnp.bfloat16)
    return block.astype(jnp.float32).T


def store_split(ref, slot, at_rows, at_lanes, value):
    high = value.astype(jnp.bfloat16)
    ref[2 * slot, at_rows, at_lanes] = high
    ref[2 * slot + 1, at_rows, at_lanes] = (value - high.astype(jnp.float32)).astype(jnp.bfloat16)


def kernel(
    members, devices,
    signal_hbm, cot_hbm, taps_hbm, proj_hbm, forward_hbm, inverse_hbm, lane_hbm, twist_hbm,
    input_got, filter_mid,
    forward, inverse, lane, twist, work, cots, signal_ref, taps_ref, proj_ref,
    signal_send, taps_send, grad_send, filter_send, input_send,
    signal_got, taps_got, grad_got, filter_got, filter_rows,
    outer, pieces, untwisted, spectra, send_sem, recv_sem, load_sem,
):
    member = lax.axis_index("rep")
    place = lax.axis_index("seq")
    half = lax.axis_index("chan")
    owners = members * devices
    me = member * devices + place
    rows = devices * SUB
    width = signal_ref.shape[1]
    chunk = signal_ref.shape[0] // SUB

    def device(owner, part):
        return {"rep": owner // devices, "seq": lax.rem(owner, devices), "chan": part}

    partner = device(me, 1 - half)
    sibling = (1 - member) * devices + place

    barrier = pltpu.get_barrier_semaphore()

    def others(body):
        def step(at, carry):
            body(lax.rem(me + at, owners))
            return carry

        lax.fori_loop(1, owners, step, 0)

    def others_of_member(body):
        def step(at, carry):
            body(lax.rem(place + at, devices))
            return carry

        lax.fori_loop(1, devices, step, 0)

    def others_in_waves(body):
        turns = owners // WAVES
        turn = me // WAVES
        for wave in range(WAVES):
            def step(at, carry):
                body(lax.rem(turn + at, turns) * WAVES + wave)
                return carry

            lax.fori_loop(1, turns, step, 0)

            @pl.when(lax.rem(me, WAVES) != wave)
            def _():
                body(turn * WAVES + wave)

    def greet(target):
        pl.semaphore_signal(barrier, inc=1, device_id=target, device_id_type=MESH)

    greet(partner)
    others(lambda owner: greet(device(owner, half)))

    loads = [
        pltpu.make_async_copy(source, target_ref, load_sem.at[at])
        for at, (source, target_ref) in enumerate(
            (
                (taps_hbm, taps_ref),
                (signal_hbm, signal_ref),
                (cot_hbm, cots.at[half]),
                (proj_hbm, proj_ref),
                (forward_hbm, forward),
                (lane_hbm, lane),
                (twist_hbm, twist),
                (inverse_hbm, inverse),
            )
        )
    ]
    for copy in loads:
        copy.start()

    def spread(source, target_ref):
        for j in range(SUB):
            work[pl.ds(j, width, stride=SUB), :] = source(j)
        target_ref[...] = work[...].reshape(width, SUB, LANES).astype(jnp.bfloat16)

    def block_of(ref):
        return lambda j: transposed(ref[j * chunk : (j + 1) * chunk, :])

    loads[0].wait()
    spread(block_of(taps_ref), taps_send)
    loads[1].wait()
    spread(block_of(signal_ref), signal_send)
    loads[2].wait()
    pl.semaphore_wait(barrier, owners)

    def remote(kind, source, target_ref, target):
        return pltpu.make_async_remote_copy(
            src_ref=source, dst_ref=target_ref, send_sem=send_sem.at[kind], recv_sem=recv_sem.at[kind],
            device_id=target, device_id_type=MESH,
        )

    cot_copy = remote(COT, cots.at[half], cots.at[half], partner)
    cot_copy.start()

    def exchange(kind, send_ref, got_ref, order=others):
        order(lambda owner: remote(kind, send_ref.at[owner], got_ref.at[me], device(owner, half)).start())
        pltpu.make_async_copy(send_ref.at[me], got_ref.at[me], recv_sem.at[kind]).start()

    def arrived(kind, got_ref):
        pltpu.make_async_copy(got_ref, got_ref, recv_sem.at[kind]).wait()

    def sent(kind, send_ref, count):
        part = send_ref.at[pl.ds(0, count)]
        pltpu.make_async_copy(part, part, send_sem.at[kind]).wait()

    others_of_member(
        lambda other: remote(
            TAP, taps_send.at[member * devices + other], taps_got.at[place], device(member * devices + other, half)
        ).start()
    )
    pltpu.make_async_copy(taps_send.at[me], taps_got.at[place], recv_sem.at[TAP]).start()
    exchange(SIG, signal_send, signal_got)

    loads[3].wait()
    cot_copy.wait_recv()

    def mixed(j):
        total = None
        for part in range(2):
            term = lax.dot_general(
                proj_ref[:, part * width : (part + 1) * width],
                cots[part, j * chunk : (j + 1) * chunk, :],
                (((1,), (1,)), ((), ())),
                preferred_element_type=jnp.float32,
            )
            total = term if total is None else total + term
        return total

    spread(mixed, grad_send)
    exchange(GRAD, grad_send, grad_got, others_in_waves)

    for copy in loads[4:]:
        copy.wait()

    steps = [slice(at, at + STEP) for at in range(0, rows, STEP)]
    lower = [slice(rows + at, rows + at + STEP) for at in range(0, rows, STEP)]
    real_lanes, imag_lanes = slice(0, LANES), slice(LANES, 2 * LANES)

    def lane_dot(slot, table):
        high, low = pieces[2 * slot], pieces[2 * slot + 1]
        return dot(jnp.concatenate([high, low, high], axis=1), lane[table])

    def transform(values, first):
        count = values.shape[1] // LANES
        outer[:, : count * LANES] = dot(forward[...], jnp.concatenate([values, values], axis=0))
        for at in range(count):
            lanes = slice(at * LANES, (at + 1) * LANES)
            slot = at % 2
            for upper_rows, lower_rows in zip(steps, lower):
                real, imag = outer[upper_rows, lanes], outer[lower_rows, lanes]
                cosine, sine = twist[0, upper_rows], twist[1, upper_rows]
                store_split(pieces, slot, upper_rows, real_lanes, real * cosine + imag * sine)
                store_split(pieces, slot, upper_rows, imag_lanes, imag * cosine - real * sine)
            spectra[first + at] = lane_dot(slot, 0)

    def member_rows(ref, at):
        return ref[at * devices : (at + 1) * devices].reshape(rows, LANES)

    def gathered(ref):
        return jnp.concatenate([member_rows(ref, at) for at in range(members)], axis=1)

    arrived(TAP, taps_got)
    arrived(SIG, signal_got)
    transform(jnp.concatenate([gathered(signal_got), taps_got[...].reshape(rows, LANES)], axis=1), 0)
    arrived(GRAD, grad_got)
    transform(gathered(grad_got), 3)

    def conj_product(pairs, at_rows):
        real_total = imag_total = None
        for first, second in pairs:
            first_real, first_imag = spectra[first, at_rows, real_lanes], spectra[first, at_rows, imag_lanes]
            second_real, second_imag = spectra[second, at_rows, real_lanes], spectra[second, at_rows, imag_lanes]
            real = first_real * second_real + first_imag * second_imag
            imag = first_imag * second_real - first_real * second_imag
            real_total = real if real_total is None else real_total + real
            imag_total = imag if imag_total is None else imag_total + imag
        return real_total, imag_total

    def untransform(pairs, slot, lanes):
        for upper_rows in steps:
            real, imag = conj_product(pairs, upper_rows)
            store_split(pieces, slot, upper_rows, real_lanes, real)
            store_split(pieces, slot, upper_rows, imag_lanes, imag)
        outer[:rows, : 2 * LANES] = lane_dot(slot, 1)
        for upper_rows, lower_rows in zip(steps, lower):
            real, imag = outer[upper_rows, real_lanes], outer[upper_rows, imag_lanes]
            cosine, sine = twist[0, upper_rows], twist[1, upper_rows]
            store_split(untwisted, 0, upper_rows, lanes, real * cosine - imag * sine)
            store_split(untwisted, 0, lower_rows, lanes, imag * cosine + real * sine)

    def rows_inverse(lanes):
        high, low = untwisted[0, :, lanes], untwisted[1, :, lanes]
        table = jnp.concatenate([inverse[0], inverse[0], inverse[1]], axis=1)
        return dot(table, jnp.concatenate([high, low, high], axis=0)).astype(jnp.bfloat16)

    untransform(((3, 0), (4, 1)), 0, slice(0, LANES))
    filter_send[...] = rows_inverse(slice(0, LANES)).reshape(devices, SUB, LANES)
    others_of_member(
        lambda other: remote(
            FILT, filter_send.at[other], filter_got.at[member, place], device(member * devices + other, half)
        ).start()
    )
    pltpu.make_async_copy(filter_send.at[place], filter_got.at[member, place], recv_sem.at[FILT]).start()

    for at in range(members):
        untransform(((3 + at, 2),), 1 - at, slice((1 + at) * LANES, (2 + at) * LANES))
    input_rows = rows_inverse(slice(LANES, 3 * LANES))
    for at in range(members):
        input_send[at * devices : (at + 1) * devices] = input_rows[
            :, at * LANES : (at + 1) * LANES
        ].reshape(devices, SUB, LANES)
    exchange(INP, input_send, input_got)

    ours = filter_got.at[member]
    arrived(FILT, ours)
    swap = remote(SWAP, ours, ours, device(sibling, half))
    swap.start()
    cot_copy.wait_send()
    sent(TAP, taps_send, devices - 1)
    sent(SIG, signal_send, owners - 1)
    sent(GRAD, grad_send, owners - 1)
    sent(FILT, filter_send, devices - 1)
    swap.wait()
    work[...] = filter_got[...].astype(jnp.float32).reshape(width * SUB, LANES)
    for j in range(SUB):
        block = work[pl.ds(j, width, stride=SUB), :].astype(jnp.bfloat16)
        filter_rows[j * chunk : (j + 1) * chunk, :] = transposed(block).astype(jnp.bfloat16)
    keep = pltpu.make_async_copy(filter_rows, filter_mid, load_sem.at[0])
    keep.start()
    keep.wait()
    arrived(INP, input_got)
    sent(INP, input_send, owners - 1)


def finish_kernel(input_hbm, filter_hbm, input_out, filter_out, input_raw, filter_raw, work, input_done, filter_done, sems):
    copies = [
        pltpu.make_async_copy(source, target, sems.at[at])
        for at, (source, target) in enumerate(
            ((input_hbm, input_raw), (filter_hbm, filter_raw), (input_done, input_out), (filter_done, filter_out))
        )
    ]
    copies[0].start()
    copies[1].start()
    width = input_raw.shape[0]
    copies[1].wait()
    filter_done[...] = filter_raw[...].astype(jnp.float32)
    copies[3].start()
    copies[0].wait()
    work[...] = input_raw[...].astype(jnp.float32).reshape(work.shape)
    for j in range(SUB):
        block = work[pl.ds(j, width, stride=SUB), :].astype(jnp.bfloat16)
        input_done[j * LANES : (j + 1) * LANES, :] = transposed(block).astype(jnp.bfloat16)
    copies[2].start()
    copies[3].wait()
    copies[2].wait()


def per_device(inputs, cotangent, filter_taps, out_proj):
    devices = lax.axis_size("seq")
    members = lax.axis_size("rep")
    tok_rows, width = filter_taps.shape
    owners = members * devices
    rows = devices * SUB
    constants = [jnp.asarray(table) for table in tables(devices * tok_rows)]
    hbm = pl.BlockSpec(memory_space=pl.ANY)
    message = (owners, SUB, LANES)
    flat = (tok_rows, width)

    def buffers(shapes, dtype):
        return [pltpu.VMEM(shape, dtype) for shape in shapes]

    input_raw, filter_raw = pl.pallas_call(
        functools.partial(kernel, members, devices),
        out_shape=(jax.ShapeDtypeStruct(message, jnp.bfloat16), jax.ShapeDtypeStruct(flat, jnp.bfloat16)),
        in_specs=[hbm] * 8,
        out_specs=(hbm, hbm),
        scratch_shapes=[pltpu.VMEM(table.shape, table.dtype) for table in constants]
        + buffers([(width * SUB, LANES)], jnp.float32)
        + buffers(
            [(2, *flat), flat, flat, out_proj.shape]
            + [message] * 3
            + [(devices, SUB, LANES), message]
            + [message, (devices, SUB, LANES), message, (members, devices, SUB, LANES), flat],
            jnp.bfloat16,
        )
        + buffers([(2 * rows, 3 * LANES)], jnp.float32)
        + buffers([(4, rows, 2 * LANES), (2, 2 * rows, 3 * LANES)], jnp.bfloat16)
        + buffers([(5, rows, 2 * LANES)], jnp.float32)
        + [
            pltpu.SemaphoreType.DMA((KINDS,)),
            pltpu.SemaphoreType.DMA((KINDS,)),
            pltpu.SemaphoreType.DMA((8,)),
        ],
        compiler_params=pltpu.CompilerParams(
            collective_id=0, has_side_effects=True, vmem_limit_bytes=VMEM_LIMIT
        ),
        name="correlate",
    )(inputs.reshape(flat), cotangent.reshape(flat), filter_taps, out_proj, *constants)
    grad_input, grad_filter = pl.pallas_call(
        finish_kernel,
        out_shape=(jax.ShapeDtypeStruct(flat, jnp.bfloat16), jax.ShapeDtypeStruct(flat, jnp.float32)),
        in_specs=[hbm] * 2,
        out_specs=(hbm, hbm),
        scratch_shapes=buffers([message, flat], jnp.bfloat16)
        + buffers([(width * SUB, LANES)], jnp.float32)
        + buffers([flat], jnp.bfloat16)
        + buffers([flat], jnp.float32)
        + [pltpu.SemaphoreType.DMA((4,))],
        compiler_params=pltpu.CompilerParams(vmem_limit_bytes=VMEM_LIMIT),
        name="finish",
    )(input_raw, filter_raw)
    return (grad_input.reshape(1, tok_rows, width), grad_filter)


def solution(mesh):
    return jax.shard_map(
        per_device,
        mesh=mesh,
        in_specs=(
            P("rep", "seq", "chan"),
            P("rep", "seq", "chan"),
            P("seq", "chan"),
            P("chan", None),
        ),
        out_specs=(P("rep", "seq", "chan"), P("seq", "chan")),
        check_vma=False,
    )
```

```python
import functools
import math

import jax
import jax.numpy as jnp
import numpy as np
from jax import lax
from jax.experimental import pallas as pl
from jax.experimental.pallas import tpu as pltpu
from jax.sharding import PartitionSpec as P

LANES = 128
SUB = 8
STEP = 128
WAVES = 2
VMEM_LIMIT = 60 * 1024 * 1024
MESH = pl.DeviceIdType.MESH
COT, SIG, TAP, GRAD, FILT, INP, SWAP = range(7)
KINDS = 7


def split_high_low(table):
    high = np.asarray(table, np.float32).astype(jnp.bfloat16)
    low = (table - high.astype(np.float64)).astype(np.float32).astype(jnp.bfloat16)
    return np.stack([high, low])


def tables(length):
    rows = length // LANES
    row_index = np.arange(rows)
    lane_index = np.arange(LANES)
    row_angle = ((4 * row_index[:, None] + 1) * row_index[None, :] % (4 * rows)) * (2.0 * math.pi / (4 * rows))
    twist_angle = ((4 * row_index[:, None] + 1) * lane_index[None, :] % (4 * length)) * (2.0 * math.pi / (4 * length))
    lane_angle = (lane_index[:, None] * lane_index[None, :] % LANES) * (2.0 * math.pi / LANES)
    row_forward = np.concatenate([np.cos(row_angle), -np.sin(row_angle)], axis=0)
    lane_cos, lane_sin = np.cos(lane_angle), np.sin(lane_angle)
    lane_forward = np.block([[lane_cos, -lane_sin], [lane_sin, lane_cos]])
    lane_inverse = np.block([[lane_cos, lane_sin], [-lane_sin, lane_cos]])
    forward_high, forward_low = split_high_low(row_forward)
    lane_tables = []
    for table in (lane_forward, lane_inverse):
        high, low = split_high_low(table)
        lane_tables.append(np.concatenate([high, high, low], axis=0))
    return (
        np.concatenate([forward_high, forward_low], axis=1),
        np.concatenate(list(split_high_low(row_forward.T / length)), axis=1),
        np.stack(lane_tables),
        np.stack([np.cos(twist_angle), np.sin(twist_angle)]).astype(np.float32),
    )


def dot(left, right):
    return jnp.dot(left, right, preferred_element_type=jnp.float32)


def transposed(block):
    at_row = lax.broadcasted_iota(jnp.int32, block.shape, 0)
    at_lane = lax.broadcasted_iota(jnp.int32, block.shape, 1)
    identity = jnp.where(at_row == at_lane, 1.0, 0.0).astype(jnp.bfloat16)
    return block.astype(jnp.float32).T


def store_split(ref, slot, at_rows, at_lanes, value):
    high = value.astype(jnp.bfloat16)
    ref[2 * slot, at_rows, at_lanes] = high
    ref[2 * slot + 1, at_rows, at_lanes] = (value - high.astype(jnp.float32)).astype(jnp.bfloat16)


def kernel(
    members, devices,
    signal_hbm, cot_hbm, taps_hbm, proj_hbm, forward_hbm, inverse_hbm, lane_hbm, twist_hbm,
    input_got, filter_mid,
    forward, inverse, lane, twist, work, cots, signal_ref, taps_ref, proj_ref,
    signal_send, taps_send, grad_send, filter_send, input_send,
    signal_got, taps_got, grad_got, filter_got, filter_rows,
    outer, pieces, untwisted, spectra, send_sem, recv_sem, load_sem,
):
    member = lax.axis_index("rep")
    place = lax.axis_index("seq")
    half = lax.axis_index("chan")
    owners = members * devices
    me = member * devices + place
    rows = devices * SUB
    width = signal_ref.shape[1]
    chunk = signal_ref.shape[0] // SUB

    other_member = 1 - member

    def device(at_member, at_place, part):
        return {"rep": at_member, "seq": at_place, "chan": part}

    def around(start, count, first, body):
        def step(at, carry):
            body(lax.rem(start + at, count))
            return carry

        lax.fori_loop(first, count, step, 0)

    barrier = pltpu.get_barrier_semaphore()

    def others(body):
        around(place, devices, 1, lambda at_place: body(member, at_place))
        around(place, devices, 0, lambda at_place: body(other_member, at_place))

    def others_of_member(body):
        around(place, devices, 1, body)

    def others_in_waves(body):
        turns = devices // WAVES
        turn = place // WAVES
        for wave in range(WAVES):
            around(turn, turns, 1, lambda at: body(member, at * WAVES + wave))

            @pl.when(lax.rem(place, WAVES) != wave)
            def _():
                body(member, turn * WAVES + wave)

            around(turn, turns, 0, lambda at: body(other_member, at * WAVES + wave))

    def greet(target):
        pl.semaphore_signal(barrier, inc=1, device_id=target, device_id_type=MESH)

    greet(device(member, place, 1 - half))
    others(lambda at_member, at_place: greet(device(at_member, at_place, half)))

    loads = [
        pltpu.make_async_copy(source, target_ref, load_sem.at[at])
        for at, (source, target_ref) in enumerate(
            (
                (taps_hbm, taps_ref),
                (signal_hbm, signal_ref),
                (cot_hbm, cots.at[half]),
                (proj_hbm, proj_ref),
                (forward_hbm, forward),
                (lane_hbm, lane),
                (twist_hbm, twist),
                (inverse_hbm, inverse),
            )
        )
    ]
    for copy in loads:
        copy.start()

    def spread(source, target_ref):
        for j in range(SUB):
            work[pl.ds(j, width, stride=SUB), :] = source(j)
        target_ref[...] = work[...].reshape(width, SUB, LANES).astype(jnp.bfloat16)

    def block_of(ref):
        return lambda j: transposed(ref[j * chunk : (j + 1) * chunk, :])

    loads[0].wait()
    spread(block_of(taps_ref), taps_send)
    loads[1].wait()
    spread(block_of(signal_ref), signal_send)
    loads[2].wait()
    pl.semaphore_wait(barrier, owners)

    def remote(kind, source, target_ref, target):
        return pltpu.make_async_remote_copy(
            src_ref=source, dst_ref=target_ref, send_sem=send_sem.at[kind], recv_sem=recv_sem.at[kind],
            device_id=target, device_id_type=MESH,
        )

    cot_copy = remote(COT, cots.at[half], cots.at[half], device(member, place, 1 - half))
    cot_copy.start()

    def exchange(kind, send_ref, got_ref, order=others):
        order(
            lambda at_member, at_place: remote(
                kind, send_ref.at[at_member * devices + at_place], got_ref.at[me], device(at_member, at_place, half)
            ).start()
        )
        pltpu.make_async_copy(send_ref.at[me], got_ref.at[me], recv_sem.at[kind]).start()

    def arrived(kind, got_ref):
        pltpu.make_async_copy(got_ref, got_ref, recv_sem.at[kind]).wait()

    def sent(kind, send_ref, count):
        part = send_ref.at[pl.ds(0, count)]
        pltpu.make_async_copy(part, part, send_sem.at[kind]).wait()

    others_of_member(
        lambda other: remote(
            TAP, taps_send.at[member * devices + other], taps_got.at[place], device(member, other, half)
        ).start()
    )
    pltpu.make_async_copy(taps_send.at[me], taps_got.at[place], recv_sem.at[TAP]).start()
    exchange(SIG, signal_send, signal_got)

    loads[3].wait()
    cot_copy.wait_recv()

    def mixed(j):
        total = None
        for part in range(2):
            term = lax.dot_general(
                proj_ref[:, part * width : (part + 1) * width],
                cots[part, j * chunk : (j + 1) * chunk, :],
                (((1,), (1,)), ((), ())),
                preferred_element_type=jnp.float32,
            )
            total = term if total is None else total + term
        return total

    spread(mixed, grad_send)
    exchange(GRAD, grad_send, grad_got, others_in_waves)

    for copy in loads[4:]:
        copy.wait()

    steps = [slice(at, at + STEP) for at in range(0, rows, STEP)]
    lower = [slice(rows + at, rows + at + STEP) for at in range(0, rows, STEP)]
    real_lanes, imag_lanes = slice(0, LANES), slice(LANES, 2 * LANES)

    def lane_dot(slot, table):
        high, low = pieces[2 * slot], pieces[2 * slot + 1]
        return dot(jnp.concatenate([high, low, high], axis=1), lane[table])

    def transform(values, first):
        count = values.shape[1] // LANES
        outer[:, : count * LANES] = dot(forward[...], jnp.concatenate([values, values], axis=0))
        for at in range(count):
            lanes = slice(at * LANES, (at + 1) * LANES)
            slot = at % 2
            for upper_rows, lower_rows in zip(steps, lower):
                real, imag = outer[upper_rows, lanes], outer[lower_rows, lanes]
                cosine, sine = twist[0, upper_rows], twist[1, upper_rows]
                store_split(pieces, slot, upper_rows, real_lanes, real * cosine + imag * sine)
                store_split(pieces, slot, upper_rows, imag_lanes, imag * cosine - real * sine)
            spectra[first + at] = lane_dot(slot, 0)

    def member_rows(ref, at):
        return ref[at * devices : (at + 1) * devices].reshape(rows, LANES)

    def gathered(ref):
        return jnp.concatenate([member_rows(ref, at) for at in range(members)], axis=1)

    arrived(TAP, taps_got)
    arrived(SIG, signal_got)
    transform(jnp.concatenate([gathered(signal_got), taps_got[...].reshape(rows, LANES)], axis=1), 0)
    arrived(GRAD, grad_got)
    transform(gathered(grad_got), 3)

    def conj_product(pairs, at_rows):
        real_total = imag_total = None
        for first, second in pairs:
            first_real, first_imag = spectra[first, at_rows, real_lanes], spectra[first, at_rows, imag_lanes]
            second_real, second_imag = spectra[second, at_rows, real_lanes], spectra[second, at_rows, imag_lanes]
            real = first_real * second_real + first_imag * second_imag
            imag = first_imag * second_real - first_real * second_imag
            real_total = real if real_total is None else real_total + real
            imag_total = imag if imag_total is None else imag_total + imag
        return real_total, imag_total

    def untransform(pairs, slot, lanes):
        for upper_rows in steps:
            real, imag = conj_product(pairs, upper_rows)
            pieces[2 * slot, upper_rows, real_lanes] = real.astype(jnp.bfloat16)
            pieces[2 * slot, upper_rows, imag_lanes] = imag.astype(jnp.bfloat16)
        high = pieces[2 * slot]
        outer[:rows, : 2 * LANES] = dot(jnp.concatenate([high, high], axis=1), lane[1, 2 * LANES :])
        for upper_rows, lower_rows in zip(steps, lower):
            real, imag = outer[upper_rows, real_lanes], outer[upper_rows, imag_lanes]
            cosine, sine = twist[0, upper_rows], twist[1, upper_rows]
            untwisted[upper_rows, lanes] = (real * cosine - imag * sine).astype(jnp.bfloat16)
            untwisted[lower_rows, lanes] = (imag * cosine + real * sine).astype(jnp.bfloat16)

    def rows_inverse(lanes):
        values = untwisted[:, lanes]
        return dot(inverse[...], jnp.concatenate([values, values], axis=0)).astype(jnp.bfloat16)

    untransform(((3, 0), (4, 1)), 0, slice(0, LANES))
    filter_send[...] = rows_inverse(slice(0, LANES)).reshape(devices, SUB, LANES)
    others_of_member(
        lambda other: remote(
            FILT, filter_send.at[other], filter_got.at[member, place], device(member, other, half)
        ).start()
    )
    pltpu.make_async_copy(filter_send.at[place], filter_got.at[member, place], recv_sem.at[FILT]).start()

    for at in range(members):
        untransform(((3 + at, 2),), 1 - at, slice((1 + at) * LANES, (2 + at) * LANES))
    input_rows = rows_inverse(slice(LANES, 3 * LANES))
    for at in range(members):
        input_send[at * devices : (at + 1) * devices] = input_rows[
            :, at * LANES : (at + 1) * LANES
        ].reshape(devices, SUB, LANES)
    exchange(INP, input_send, input_got)

    ours = filter_got.at[member]
    arrived(FILT, ours)
    swap = remote(SWAP, ours, ours, device(other_member, place, half))
    swap.start()
    cot_copy.wait_send()
    sent(TAP, taps_send, devices - 1)
    sent(SIG, signal_send, owners - 1)
    sent(GRAD, grad_send, owners - 1)
    sent(FILT, filter_send, devices - 1)
    swap.wait()
    work[...] = filter_got[...].astype(jnp.float32).reshape(width * SUB, LANES)
    for j in range(SUB):
        block = work[pl.ds(j, width, stride=SUB), :].astype(jnp.bfloat16)
        filter_rows[j * chunk : (j + 1) * chunk, :] = transposed(block).astype(jnp.bfloat16)
    keep = pltpu.make_async_copy(filter_rows, filter_mid, load_sem.at[0])
    keep.start()
    keep.wait()
    arrived(INP, input_got)
    sent(INP, input_send, owners - 1)


def finish_kernel(input_hbm, filter_hbm, input_out, filter_out, input_raw, filter_raw, work, input_done, filter_done, sems):
    copies = [
        pltpu.make_async_copy(source, target, sems.at[at])
        for at, (source, target) in enumerate(
            ((input_hbm, input_raw), (filter_hbm, filter_raw), (input_done, input_out), (filter_done, filter_out))
        )
    ]
    copies[0].start()
    copies[1].start()
    width = input_raw.shape[0]
    copies[1].wait()
    filter_done[...] = filter_raw[...].astype(jnp.float32)
    copies[3].start()
    copies[0].wait()
    work[...] = input_raw[...].astype(jnp.float32).reshape(work.shape)
    for j in range(SUB):
        block = work[pl.ds(j, width, stride=SUB), :].astype(jnp.bfloat16)
        input_done[j * LANES : (j + 1) * LANES, :] = transposed(block).astype(jnp.bfloat16)
    copies[2].start()
    copies[3].wait()
    copies[2].wait()


def per_device(inputs, cotangent, filter_taps, out_proj):
    devices = lax.axis_size("seq")
    members = lax.axis_size("rep")
    tok_rows, width = filter_taps.shape
    owners = members * devices
    rows = devices * SUB
    constants = [jnp.asarray(table) for table in tables(devices * tok_rows)]
    hbm = pl.BlockSpec(memory_space=pl.ANY)
    message = (owners, SUB, LANES)
    flat = (tok_rows, width)

    def buffers(shapes, dtype):
        return [pltpu.VMEM(shape, dtype) for shape in shapes]

    input_raw, filter_raw = pl.pallas_call(
        functools.partial(kernel, members, devices),
        out_shape=(jax.ShapeDtypeStruct(message, jnp.bfloat16), jax.ShapeDtypeStruct(flat, jnp.bfloat16)),
        in_specs=[hbm] * 8,
        out_specs=(hbm, hbm),
        scratch_shapes=[pltpu.VMEM(table.shape, table.dtype) for table in constants]
        + buffers([(width * SUB, LANES)], jnp.float32)
        + buffers(
            [(2, *flat), flat, flat, out_proj.shape]
            + [message] * 3
            + [(devices, SUB, LANES), message]
            + [message, (devices, SUB, LANES), message, (members, devices, SUB, LANES), flat],
            jnp.bfloat16,
        )
        + buffers([(2 * rows, 3 * LANES)], jnp.float32)
        + buffers([(4, rows, 2 * LANES), (2 * rows, 3 * LANES)], jnp.bfloat16)
        + buffers([(5, rows, 2 * LANES)], jnp.float32)
        + [
            pltpu.SemaphoreType.DMA((KINDS,)),
            pltpu.SemaphoreType.DMA((KINDS,)),
            pltpu.SemaphoreType.DMA((8,)),
        ],
        compiler_params=pltpu.CompilerParams(
            collective_id=0, has_side_effects=True, vmem_limit_bytes=VMEM_LIMIT
        ),
        name="correlate",
    )(inputs.reshape(flat), cotangent.reshape(flat), filter_taps, out_proj, *constants)
    grad_input, grad_filter = pl.pallas_call(
        finish_kernel,
        out_shape=(jax.ShapeDtypeStruct(flat, jnp.bfloat16), jax.ShapeDtypeStruct(flat, jnp.float32)),
        in_specs=[hbm] * 2,
        out_specs=(hbm, hbm),
        scratch_shapes=buffers([message, flat], jnp.bfloat16)
        + buffers([(width * SUB, LANES)], jnp.float32)
        + buffers([flat], jnp.bfloat16)
        + buffers([flat], jnp.float32)
        + [pltpu.SemaphoreType.DMA((4,))],
        compiler_params=pltpu.CompilerParams(vmem_limit_bytes=VMEM_LIMIT),
        name="finish",
    )(input_raw, filter_raw)
    return (grad_input.reshape(1, tok_rows, width), grad_filter)


def solution(mesh):
    return jax.shard_map(
        per_device,
        mesh=mesh,
        in_specs=(
            P("rep", "seq", "chan"),
            P("rep", "seq", "chan"),
            P("seq", "chan"),
            P("chan", None),
        ),
        out_specs=(P("rep", "seq", "chan"), P("seq", "chan")),
        check_vma=False,
    )
```

```python
import functools
import math

import jax
import jax.numpy as jnp
import numpy as np
from jax import lax
from jax.experimental import pallas as pl
from jax.experimental.pallas import tpu as pltpu
from jax.sharding import PartitionSpec as P

LANES = 128
SUB = 8
STEP = 128
WAVES = 2
VMEM_LIMIT = 60 * 1024 * 1024
MESH = pl.DeviceIdType.MESH
COT, SIG, TAP, GRAD, FILT, INP, SWAP = range(7)
KINDS = 7


def split_high_low(table):
    high = np.asarray(table, np.float32).astype(jnp.bfloat16)
    low = (table - high.astype(np.float64)).astype(np.float32).astype(jnp.bfloat16)
    return np.stack([high, low])


def tables(length):
    rows = length // LANES
    row_index = np.arange(rows)
    lane_index = np.arange(LANES)
    row_angle = ((4 * row_index[:, None] + 1) * row_index[None, :] % (4 * rows)) * (2.0 * math.pi / (4 * rows))
    twist_angle = ((4 * row_index[:, None] + 1) * lane_index[None, :] % (4 * length)) * (2.0 * math.pi / (4 * length))
    lane_angle = (lane_index[:, None] * lane_index[None, :] % LANES) * (2.0 * math.pi / LANES)
    row_forward = np.concatenate([np.cos(row_angle), -np.sin(row_angle)], axis=0)
    lane_cos, lane_sin = np.cos(lane_angle), np.sin(lane_angle)
    lane_forward = np.block([[lane_cos, -lane_sin], [lane_sin, lane_cos]])
    lane_inverse = np.block([[lane_cos, lane_sin], [-lane_sin, lane_cos]])
    forward_high, forward_low = split_high_low(row_forward)
    lane_tables = []
    for table in (lane_forward, lane_inverse):
        high, low = split_high_low(table)
        lane_tables.append(np.concatenate([high, high, low], axis=0))
    return (
        np.concatenate([forward_high, forward_low], axis=1),
        np.concatenate(list(split_high_low(row_forward.T / length)), axis=1),
        np.stack(lane_tables),
        np.stack([np.cos(twist_angle), np.sin(twist_angle)]).astype(np.float32),
    )


def dot(left, right):
    return jnp.dot(left, right, preferred_element_type=jnp.float32)


def transposed(block):
    at_row = lax.broadcasted_iota(jnp.int32, block.shape, 0)
    at_lane = lax.broadcasted_iota(jnp.int32, block.shape, 1)
    identity = jnp.where(at_row == at_lane, 1.0, 0.0).astype(jnp.bfloat16)
    return block.astype(jnp.float32).T


def store_split(ref, slot, at_rows, at_lanes, value):
    high = value.astype(jnp.bfloat16)
    ref[2 * slot, at_rows, at_lanes] = high
    ref[2 * slot + 1, at_rows, at_lanes] = (value - high.astype(jnp.float32)).astype(jnp.bfloat16)


def kernel(
    members, devices,
    signal_hbm, cot_hbm, taps_hbm, proj_hbm, forward_hbm, inverse_hbm, lane_hbm, twist_hbm,
    input_got, filter_mid,
    forward, inverse, lane, twist, work, cots, signal_ref, taps_ref, proj_ref,
    signal_send, taps_send, grad_send, filter_send, input_send,
    signal_got, taps_got, grad_got, filter_got, filter_rows,
    outer, pieces, untwisted, spectra, send_sem, recv_sem, load_sem,
):
    member = lax.axis_index("rep")
    place = lax.axis_index("seq")
    half = lax.axis_index("chan")
    owners = members * devices
    me = member * devices + place
    rows = devices * SUB
    width = signal_ref.shape[1]
    chunk = signal_ref.shape[0] // SUB

    other_member = 1 - member

    def device(at_member, at_place, part):
        return {"rep": at_member, "seq": at_place, "chan": part}

    def around(start, count, first, body):
        def step(at, carry):
            body(lax.rem(start + at, count))
            return carry

        lax.fori_loop(first, count, step, 0)

    barrier = pltpu.get_barrier_semaphore()

    def others(body):
        around(place, devices, 1, lambda at_place: body(member, at_place))
        around(place, devices, 0, lambda at_place: body(other_member, at_place))

    def others_of_member(body):
        around(place, devices, 1, body)

    def others_in_waves(body):
        turns = devices // WAVES
        turn = place // WAVES
        for wave in range(WAVES):
            around(turn, turns, 1, lambda at: body(member, at * WAVES + wave))

            @pl.when(lax.rem(place, WAVES) != wave)
            def _():
                body(member, turn * WAVES + wave)

            around(turn, turns, 0, lambda at: body(other_member, at * WAVES + wave))

    def greet(target):
        pl.semaphore_signal(barrier, inc=1, device_id=target, device_id_type=MESH)

    greet(device(member, place, 1 - half))
    others(lambda at_member, at_place: greet(device(at_member, at_place, half)))

    loads = [
        pltpu.make_async_copy(source, target_ref, load_sem.at[at])
        for at, (source, target_ref) in enumerate(
            (
                (taps_hbm, taps_ref),
                (signal_hbm, signal_ref),
                (cot_hbm, cots.at[half]),
                (proj_hbm, proj_ref),
                (forward_hbm, forward),
                (lane_hbm, lane),
                (twist_hbm, twist),
                (inverse_hbm, inverse),
            )
        )
    ]
    for copy in loads:
        copy.start()

    def spread(source, target_ref):
        for j in range(SUB):
            work[pl.ds(j, width, stride=SUB), :] = source(j)
        target_ref[...] = work[...].reshape(width, SUB, LANES).astype(jnp.bfloat16)

    def block_of(ref):
        return lambda j: transposed(ref[j * chunk : (j + 1) * chunk, :])

    loads[0].wait()
    spread(block_of(taps_ref), taps_send)
    loads[1].wait()
    spread(block_of(signal_ref), signal_send)
    loads[2].wait()
    pl.semaphore_wait(barrier, owners)

    def remote(kind, source, target_ref, target):
        return pltpu.make_async_remote_copy(
            src_ref=source, dst_ref=target_ref, send_sem=send_sem.at[kind], recv_sem=recv_sem.at[kind],
            device_id=target, device_id_type=MESH,
        )

    cot_copy = remote(COT, cots.at[half], cots.at[half], device(member, place, 1 - half))
    cot_copy.start()

    def exchange(kind, send_ref, got_ref, order=others):
        order(
            lambda at_member, at_place: remote(
                kind, send_ref.at[at_member * devices + at_place], got_ref.at[me], device(at_member, at_place, half)
            ).start()
        )
        pltpu.make_async_copy(send_ref.at[me], got_ref.at[me], recv_sem.at[kind]).start()

    def arrived(kind, got_ref):
        pltpu.make_async_copy(got_ref, got_ref, recv_sem.at[kind]).wait()

    def sent(kind, send_ref, count):
        part = send_ref.at[pl.ds(0, count)]
        pltpu.make_async_copy(part, part, send_sem.at[kind]).wait()

    others_of_member(
        lambda other: remote(
            TAP, taps_send.at[member * devices + other], taps_got.at[place], device(member, other, half)
        ).start()
    )
    pltpu.make_async_copy(taps_send.at[me], taps_got.at[place], recv_sem.at[TAP]).start()
    exchange(SIG, signal_send, signal_got)

    loads[3].wait()
    cot_copy.wait_recv()

    def mixed(j):
        total = None
        for part in range(2):
            term = lax.dot_general(
                proj_ref[:, part * width : (part + 1) * width],
                cots[part, j * chunk : (j + 1) * chunk, :],
                (((1,), (1,)), ((), ())),
                preferred_element_type=jnp.float32,
            )
            total = term if total is None else total + term
        return total

    spread(mixed, grad_send)
    exchange(GRAD, grad_send, grad_got, others_in_waves)

    for copy in loads[4:]:
        copy.wait()

    steps = [slice(at, at + STEP) for at in range(0, rows, STEP)]
    lower = [slice(rows + at, rows + at + STEP) for at in range(0, rows, STEP)]
    real_lanes, imag_lanes = slice(0, LANES), slice(LANES, 2 * LANES)

    def lane_dot(slot, table):
        high, low = pieces[2 * slot], pieces[2 * slot + 1]
        return dot(jnp.concatenate([high, low, high], axis=1), lane[table])

    def transform(values, first):
        count = values.shape[1] // LANES
        outer[:, : count * LANES] = dot(forward[...], jnp.concatenate([values, values], axis=0))
        for at in range(count):
            lanes = slice(at * LANES, (at + 1) * LANES)
            slot = at % 2
            for upper_rows, lower_rows in zip(steps, lower):
                real, imag = outer[upper_rows, lanes], outer[lower_rows, lanes]
                cosine, sine = twist[0, upper_rows], twist[1, upper_rows]
                store_split(pieces, slot, upper_rows, real_lanes, real * cosine + imag * sine)
                store_split(pieces, slot, upper_rows, imag_lanes, imag * cosine - real * sine)
            spectra[first + at] = lane_dot(slot, 0)

    def member_rows(ref, at):
        return ref[at * devices : (at + 1) * devices].reshape(rows, LANES)

    def gathered(ref):
        return jnp.concatenate([member_rows(ref, at) for at in range(members)], axis=1)

    arrived(TAP, taps_got)
    arrived(SIG, signal_got)
    transform(jnp.concatenate([gathered(signal_got), taps_got[...].reshape(rows, LANES)], axis=1), 0)
    arrived(GRAD, grad_got)
    transform(gathered(grad_got), 3)

    def conj_product(pairs, at_rows):
        real_total = imag_total = None
        for first, second in pairs:
            first_real, first_imag = spectra[first, at_rows, real_lanes], spectra[first, at_rows, imag_lanes]
            second_real, second_imag = spectra[second, at_rows, real_lanes], spectra[second, at_rows, imag_lanes]
            real = first_real * second_real + first_imag * second_imag
            imag = first_imag * second_real - first_real * second_imag
            real_total = real if real_total is None else real_total + real
            imag_total = imag if imag_total is None else imag_total + imag
        return real_total, imag_total

    def untransform(pairs, slot, lanes):
        for upper_rows in steps:
            real, imag = conj_product(pairs, upper_rows)
            pieces[2 * slot, upper_rows, real_lanes] = real.astype(jnp.bfloat16)
            pieces[2 * slot, upper_rows, imag_lanes] = imag.astype(jnp.bfloat16)
        high = pieces[2 * slot]
        outer[:rows, : 2 * LANES] = dot(jnp.concatenate([high, high], axis=1), lane[1, 2 * LANES :])
        for upper_rows, lower_rows in zip(steps, lower):
            real, imag = outer[upper_rows, real_lanes], outer[upper_rows, imag_lanes]
            cosine, sine = twist[0, upper_rows], twist[1, upper_rows]
            untwisted[upper_rows, lanes] = (real * cosine - imag * sine).astype(jnp.bfloat16)
            untwisted[lower_rows, lanes] = (imag * cosine + real * sine).astype(jnp.bfloat16)

    def rows_inverse(lanes):
        values = untwisted[:, lanes]
        return dot(inverse[...], jnp.concatenate([values, values], axis=0)).astype(jnp.bfloat16)

    untransform(((3, 0), (4, 1)), 0, slice(0, LANES))
    filter_send[...] = rows_inverse(slice(0, LANES)).reshape(devices, SUB, LANES)
    others_of_member(
        lambda other: remote(
            FILT, filter_send.at[other], filter_got.at[member, place], device(member, other, half)
        ).start()
    )
    pltpu.make_async_copy(filter_send.at[place], filter_got.at[member, place], recv_sem.at[FILT]).start()

    for turn in range(members):
        at = other_member if turn else member
        lanes = slice((1 + turn) * LANES, (2 + turn) * LANES)
        untransform(((3 + at, 2),), 1 - turn, lanes)
        input_send[pl.ds(at * devices, devices)] = rows_inverse(lanes).reshape(devices, SUB, LANES)

        def send_input(at_place, at=at):
            remote(INP, input_send.at[at * devices + at_place], input_got.at[me], device(at, at_place, half)).start()

        around(place, devices, 0 if turn else 1, send_input)
    pltpu.make_async_copy(input_send.at[me], input_got.at[me], recv_sem.at[INP]).start()

    ours = filter_got.at[member]
    arrived(FILT, ours)
    swap = remote(SWAP, ours, ours, device(other_member, place, half))
    swap.start()
    cot_copy.wait_send()
    sent(TAP, taps_send, devices - 1)
    sent(SIG, signal_send, owners - 1)
    sent(GRAD, grad_send, owners - 1)
    sent(FILT, filter_send, devices - 1)
    swap.wait()
    work[...] = filter_got[...].astype(jnp.float32).reshape(width * SUB, LANES)
    for j in range(SUB):
        block = work[pl.ds(j, width, stride=SUB), :].astype(jnp.bfloat16)
        filter_rows[j * chunk : (j + 1) * chunk, :] = transposed(block).astype(jnp.bfloat16)
    keep = pltpu.make_async_copy(filter_rows, filter_mid, load_sem.at[0])
    keep.start()
    keep.wait()
    arrived(INP, input_got)
    sent(INP, input_send, owners - 1)


def finish_kernel(input_hbm, filter_hbm, input_out, filter_out, input_raw, filter_raw, work, input_done, filter_done, sems):
    copies = [
        pltpu.make_async_copy(source, target, sems.at[at])
        for at, (source, target) in enumerate(
            ((input_hbm, input_raw), (filter_hbm, filter_raw), (input_done, input_out), (filter_done, filter_out))
        )
    ]
    copies[0].start()
    copies[1].start()
    width = input_raw.shape[0]
    copies[1].wait()
    filter_done[...] = filter_raw[...].astype(jnp.float32)
    copies[3].start()
    copies[0].wait()
    work[...] = input_raw[...].astype(jnp.float32).reshape(work.shape)
    for j in range(SUB):
        block = work[pl.ds(j, width, stride=SUB), :].astype(jnp.bfloat16)
        input_done[j * LANES : (j + 1) * LANES, :] = transposed(block).astype(jnp.bfloat16)
    copies[2].start()
    copies[3].wait()
    copies[2].wait()


def per_device(inputs, cotangent, filter_taps, out_proj):
    devices = lax.axis_size("seq")
    members = lax.axis_size("rep")
    tok_rows, width = filter_taps.shape
    owners = members * devices
    rows = devices * SUB
    constants = [jnp.asarray(table) for table in tables(devices * tok_rows)]
    hbm = pl.BlockSpec(memory_space=pl.ANY)
    message = (owners, SUB, LANES)
    flat = (tok_rows, width)

    def buffers(shapes, dtype):
        return [pltpu.VMEM(shape, dtype) for shape in shapes]

    input_raw, filter_raw = pl.pallas_call(
        functools.partial(kernel, members, devices),
        out_shape=(jax.ShapeDtypeStruct(message, jnp.bfloat16), jax.ShapeDtypeStruct(flat, jnp.bfloat16)),
        in_specs=[hbm] * 8,
        out_specs=(hbm, hbm),
        scratch_shapes=[pltpu.VMEM(table.shape, table.dtype) for table in constants]
        + buffers([(width * SUB, LANES)], jnp.float32)
        + buffers(
            [(2, *flat), flat, flat, out_proj.shape]
            + [message] * 3
            + [(devices, SUB, LANES), message]
            + [message, (devices, SUB, LANES), message, (members, devices, SUB, LANES), flat],
            jnp.bfloat16,
        )
        + buffers([(2 * rows, 3 * LANES)], jnp.float32)
        + buffers([(4, rows, 2 * LANES), (2 * rows, 3 * LANES)], jnp.bfloat16)
        + buffers([(5, rows, 2 * LANES)], jnp.float32)
        + [
            pltpu.SemaphoreType.DMA((KINDS,)),
            pltpu.SemaphoreType.DMA((KINDS,)),
            pltpu.SemaphoreType.DMA((8,)),
        ],
        compiler_params=pltpu.CompilerParams(
            collective_id=0, has_side_effects=True, vmem_limit_bytes=VMEM_LIMIT
        ),
        name="correlate",
    )(inputs.reshape(flat), cotangent.reshape(flat), filter_taps, out_proj, *constants)
    grad_input, grad_filter = pl.pallas_call(
        finish_kernel,
        out_shape=(jax.ShapeDtypeStruct(flat, jnp.bfloat16), jax.ShapeDtypeStruct(flat, jnp.float32)),
        in_specs=[hbm] * 2,
        out_specs=(hbm, hbm),
        scratch_shapes=buffers([message, flat], jnp.bfloat16)
        + buffers([(width * SUB, LANES)], jnp.float32)
        + buffers([flat], jnp.bfloat16)
        + buffers([flat], jnp.float32)
        + [pltpu.SemaphoreType.DMA((4,))],
        compiler_params=pltpu.CompilerParams(vmem_limit_bytes=VMEM_LIMIT),
        name="finish",
    )(input_raw, filter_raw)
    return (grad_input.reshape(1, tok_rows, width), grad_filter)


def solution(mesh):
    return jax.shard_map(
        per_device,
        mesh=mesh,
        in_specs=(
            P("rep", "seq", "chan"),
            P("rep", "seq", "chan"),
            P("seq", "chan"),
            P("chan", None),
        ),
        out_specs=(P("rep", "seq", "chan"), P("seq", "chan")),
        check_vma=False,
    )
```

```python
import functools
import math

import jax
import jax.numpy as jnp
import numpy as np
from jax import lax
from jax.experimental import pallas as pl
from jax.experimental.pallas import tpu as pltpu
from jax.sharding import PartitionSpec as P

LANES = 128
SUB = 8
STEP = 128
WAVES = 2
PARTS = 2
VMEM_LIMIT = 60 * 1024 * 1024
MESH = pl.DeviceIdType.MESH
COT, SIG, TAP, GRAD, FILT, INP, SWAP = range(7)
KINDS = 7


def split_high_low(table):
    high = np.asarray(table, np.float32).astype(jnp.bfloat16)
    low = (table - high.astype(np.float64)).astype(np.float32).astype(jnp.bfloat16)
    return np.stack([high, low])


def tables(length):
    rows = length // LANES
    row_index = np.arange(rows)
    lane_index = np.arange(LANES)
    row_angle = ((4 * row_index[:, None] + 1) * row_index[None, :] % (4 * rows)) * (2.0 * math.pi / (4 * rows))
    twist_angle = ((4 * row_index[:, None] + 1) * lane_index[None, :] % (4 * length)) * (2.0 * math.pi / (4 * length))
    lane_angle = (lane_index[:, None] * lane_index[None, :] % LANES) * (2.0 * math.pi / LANES)
    row_forward = np.concatenate([np.cos(row_angle), -np.sin(row_angle)], axis=0)
    lane_cos, lane_sin = np.cos(lane_angle), np.sin(lane_angle)
    lane_forward = np.block([[lane_cos, -lane_sin], [lane_sin, lane_cos]])
    lane_inverse = np.block([[lane_cos, lane_sin], [-lane_sin, lane_cos]])
    forward_high, forward_low = split_high_low(row_forward)
    lane_tables = []
    for table in (lane_forward, lane_inverse):
        high, low = split_high_low(table)
        lane_tables.append(np.concatenate([high, high, low], axis=0))
    return (
        np.concatenate([forward_high, forward_low], axis=1),
        np.concatenate(list(split_high_low(row_forward.T / length)), axis=1),
        np.stack(lane_tables),
        np.stack([np.cos(twist_angle), np.sin(twist_angle)]).astype(np.float32),
    )


def dot(left, right):
    return jnp.dot(left, right, preferred_element_type=jnp.float32)


def transposed(block):
    at_row = lax.broadcasted_iota(jnp.int32, block.shape, 0)
    at_lane = lax.broadcasted_iota(jnp.int32, block.shape, 1)
    identity = jnp.where(at_row == at_lane, 1.0, 0.0).astype(jnp.bfloat16)
    return block.astype(jnp.float32).T


def store_split(ref, slot, at_rows, at_lanes, value):
    high = value.astype(jnp.bfloat16)
    ref[2 * slot, at_rows, at_lanes] = high
    ref[2 * slot + 1, at_rows, at_lanes] = (value - high.astype(jnp.float32)).astype(jnp.bfloat16)


def kernel(
    members, devices,
    signal_hbm, cot_hbm, taps_hbm, proj_hbm, forward_hbm, inverse_hbm, lane_hbm, twist_hbm,
    input_got, filter_all,
    forward, inverse, lane, twist, work, cots, signal_ref, taps_ref, proj_ref,
    signal_send, taps_send, grad_send, filter_send, input_send,
    signal_got, taps_got, grad_got, filter_got,
    outer, pieces, untwisted, spectra, send_sem, recv_sem, load_sem,
):
    member = lax.axis_index("rep")
    place = lax.axis_index("seq")
    half = lax.axis_index("chan")
    owners = members * devices
    me = member * devices + place
    rows = devices * SUB
    width = signal_ref.shape[1]
    chunk = signal_ref.shape[0] // SUB

    other_member = 1 - member

    def device(at_member, at_place, part):
        return {"rep": at_member, "seq": at_place, "chan": part}

    def around(start, count, first, body):
        def step(at, carry):
            body(lax.rem(start + at, count))
            return carry

        lax.fori_loop(first, count, step, 0)

    barrier = pltpu.get_barrier_semaphore()

    def others(body):
        around(place, devices, 1, lambda at_place: body(member, at_place))
        around(place, devices, 0, lambda at_place: body(other_member, at_place))

    def others_of_member(body):
        around(place, devices, 1, body)

    def others_in_waves(body):
        turns = devices // WAVES
        turn = place // WAVES
        for wave in range(WAVES):
            around(turn, turns, 1, lambda at: body(member, at * WAVES + wave))

            @pl.when(lax.rem(place, WAVES) != wave)
            def _():
                body(member, turn * WAVES + wave)

            around(turn, turns, 0, lambda at: body(other_member, at * WAVES + wave))

    def greet(target):
        pl.semaphore_signal(barrier, inc=1, device_id=target, device_id_type=MESH)

    greet(device(member, place, 1 - half))
    others(lambda at_member, at_place: greet(device(at_member, at_place, half)))

    loads = [
        pltpu.make_async_copy(source, target_ref, load_sem.at[at])
        for at, (source, target_ref) in enumerate(
            (
                (taps_hbm, taps_ref),
                (signal_hbm, signal_ref),
                (cot_hbm, cots.at[half]),
                (proj_hbm, proj_ref),
                (forward_hbm, forward),
                (lane_hbm, lane),
                (twist_hbm, twist),
                (inverse_hbm, inverse),
            )
        )
    ]
    for copy in loads:
        copy.start()

    def spread(source, target_ref):
        for j in range(SUB):
            work[pl.ds(j, width, stride=SUB), :] = source(j)
        target_ref[...] = work[...].reshape(width, SUB, LANES).astype(jnp.bfloat16)

    def block_of(ref):
        return lambda j: transposed(ref[j * chunk : (j + 1) * chunk, :])

    loads[0].wait()
    spread(block_of(taps_ref), taps_send)
    loads[1].wait()
    spread(block_of(signal_ref), signal_send)
    loads[2].wait()
    pl.semaphore_wait(barrier, owners)

    def remote(kind, source, target_ref, target):
        return pltpu.make_async_remote_copy(
            src_ref=source, dst_ref=target_ref, send_sem=send_sem.at[kind], recv_sem=recv_sem.at[kind],
            device_id=target, device_id_type=MESH,
        )

    cot_copy = remote(COT, cots.at[half], cots.at[half], device(member, place, 1 - half))
    cot_copy.start()

    def exchange(kind, send_ref, got_ref, order=others):
        order(
            lambda at_member, at_place: remote(
                kind, send_ref.at[at_member * devices + at_place], got_ref.at[me], device(at_member, at_place, half)
            ).start()
        )
        pltpu.make_async_copy(send_ref.at[me], got_ref.at[me], recv_sem.at[kind]).start()

    def arrived(kind, got_ref):
        pltpu.make_async_copy(got_ref, got_ref, recv_sem.at[kind]).wait()

    def sent(kind, send_ref, count):
        part = send_ref.at[pl.ds(0, count)]
        pltpu.make_async_copy(part, part, send_sem.at[kind]).wait()

    others_of_member(
        lambda other: remote(
            TAP, taps_send.at[member * devices + other], taps_got.at[place], device(member, other, half)
        ).start()
    )
    pltpu.make_async_copy(taps_send.at[me], taps_got.at[place], recv_sem.at[TAP]).start()
    exchange(SIG, signal_send, signal_got)

    loads[3].wait()
    cot_copy.wait_recv()

    def mixed(j):
        total = None
        for part in range(2):
            term = lax.dot_general(
                proj_ref[:, part * width : (part + 1) * width],
                cots[part, j * chunk : (j + 1) * chunk, :],
                (((1,), (1,)), ((), ())),
                preferred_element_type=jnp.float32,
            )
            total = term if total is None else total + term
        return total

    spread(mixed, grad_send)
    exchange(GRAD, grad_send, grad_got, others_in_waves)

    for copy in loads[4:]:
        copy.wait()

    steps = [slice(at, at + STEP) for at in range(0, rows, STEP)]
    lower = [slice(rows + at, rows + at + STEP) for at in range(0, rows, STEP)]
    real_lanes, imag_lanes = slice(0, LANES), slice(LANES, 2 * LANES)

    def lane_dot(slot, table):
        high, low = pieces[2 * slot], pieces[2 * slot + 1]
        return dot(jnp.concatenate([high, low, high], axis=1), lane[table])

    def transform(values, first):
        count = values.shape[1] // LANES
        outer[:, : count * LANES] = dot(forward[...], jnp.concatenate([values, values], axis=0))
        for at in range(count):
            lanes = slice(at * LANES, (at + 1) * LANES)
            slot = at % 2
            for upper_rows, lower_rows in zip(steps, lower):
                real, imag = outer[upper_rows, lanes], outer[lower_rows, lanes]
                cosine, sine = twist[0, upper_rows], twist[1, upper_rows]
                store_split(pieces, slot, upper_rows, real_lanes, real * cosine + imag * sine)
                store_split(pieces, slot, upper_rows, imag_lanes, imag * cosine - real * sine)
            spectra[first + at] = lane_dot(slot, 0)

    def member_rows(ref, at):
        return ref[at * devices : (at + 1) * devices].reshape(rows, LANES)

    def gathered(ref):
        return jnp.concatenate([member_rows(ref, at) for at in range(members)], axis=1)

    arrived(TAP, taps_got)
    arrived(SIG, signal_got)
    transform(jnp.concatenate([gathered(signal_got), taps_got[...].reshape(rows, LANES)], axis=1), 0)
    arrived(GRAD, grad_got)
    transform(gathered(grad_got), 3)

    def conj_product(pairs, at_rows):
        real_total = imag_total = None
        for first, second in pairs:
            first_real, first_imag = spectra[first, at_rows, real_lanes], spectra[first, at_rows, imag_lanes]
            second_real, second_imag = spectra[second, at_rows, real_lanes], spectra[second, at_rows, imag_lanes]
            real = first_real * second_real + first_imag * second_imag
            imag = first_imag * second_real - first_real * second_imag
            real_total = real if real_total is None else real_total + real
            imag_total = imag if imag_total is None else imag_total + imag
        return real_total, imag_total

    def untransform(pairs, slot, lanes):
        for upper_rows in steps:
            real, imag = conj_product(pairs, upper_rows)
            pieces[2 * slot, upper_rows, real_lanes] = real.astype(jnp.bfloat16)
            pieces[2 * slot, upper_rows, imag_lanes] = imag.astype(jnp.bfloat16)
        high = pieces[2 * slot]
        outer[:rows, : 2 * LANES] = dot(jnp.concatenate([high, high], axis=1), lane[1, 2 * LANES :])
        for upper_rows, lower_rows in zip(steps, lower):
            real, imag = outer[upper_rows, real_lanes], outer[upper_rows, imag_lanes]
            cosine, sine = twist[0, upper_rows], twist[1, upper_rows]
            untwisted[upper_rows, lanes] = (real * cosine - imag * sine).astype(jnp.bfloat16)
            untwisted[lower_rows, lanes] = (imag * cosine + real * sine).astype(jnp.bfloat16)

    def rows_inverse(lanes):
        values = untwisted[:, lanes]
        return dot(inverse[...], jnp.concatenate([values, values], axis=0)).astype(jnp.bfloat16)

    untransform(((3, 0), (4, 1)), 0, slice(0, LANES))
    filter_send[...] = rows_inverse(slice(0, LANES)).reshape(devices, SUB, LANES)
    others_of_member(
        lambda other: remote(
            FILT, filter_send.at[other], filter_got.at[place], device(member, other, half)
        ).start()
    )
    pltpu.make_async_copy(filter_send.at[place], filter_got.at[place], recv_sem.at[FILT]).start()

    for turn in range(members):
        at = other_member if turn else member
        lanes = slice((1 + turn) * LANES, (2 + turn) * LANES)
        untransform(((3 + at, 2),), 1 - turn, lanes)
        input_send[pl.ds(at * devices, devices)] = rows_inverse(lanes).reshape(devices, SUB, LANES)

        def send_input(at_place, at=at):
            remote(INP, input_send.at[at * devices + at_place], input_got.at[me], device(at, at_place, half)).start()

        around(place, devices, 0 if turn else 1, send_input)
    pltpu.make_async_copy(input_send.at[me], input_got.at[me], recv_sem.at[INP]).start()

    arrived(FILT, filter_got)
    swap = remote(SWAP, filter_got, filter_all.at[member], device(other_member, place, half))
    swap.start()
    keep = pltpu.make_async_copy(filter_got, filter_all.at[member], load_sem.at[0])
    keep.start()
    cot_copy.wait_send()
    sent(TAP, taps_send, devices - 1)
    sent(SIG, signal_send, owners - 1)
    sent(GRAD, grad_send, owners - 1)
    sent(FILT, filter_send, devices - 1)
    keep.wait()
    swap.wait()
    arrived(INP, input_got)
    sent(INP, input_send, owners - 1)


def finish_kernel(
    input_hbm, filter_hbm, input_out, filter_out,
    input_raw, filter_raw, input_work, filter_work, input_done, filter_done, load_sems, keep_sems,
):
    input_load = pltpu.make_async_copy(input_hbm, input_raw, load_sems.at[0])
    filter_load = pltpu.make_async_copy(filter_hbm, filter_raw, load_sems.at[1])
    filter_load.start()
    input_load.start()
    width = input_raw.shape[0]
    part_rows = input_out.shape[0] // PARTS
    keeps = []
    for load, raw, work, done, out in (
        (filter_load, filter_raw, filter_work, filter_done, filter_out),
        (input_load, input_raw, input_work, input_done, input_out),
    ):
        load.wait()
        work[...] = raw[...].astype(jnp.float32).reshape(work.shape)
        for j in range(SUB):
            block = work[pl.ds(j, width, stride=SUB), :]
            done[j * LANES : (j + 1) * LANES, :] = block.T.astype(done.dtype)
            if (j + 1) * LANES % part_rows == 0:
                part = pl.ds((j + 1) * LANES - part_rows, part_rows)
                keeps.append(pltpu.make_async_copy(done.at[part], out.at[part], keep_sems.at[len(keeps)]))
                keeps[-1].start()
    for keep in keeps:
        keep.wait()


def per_device(inputs, cotangent, filter_taps, out_proj):
    devices = lax.axis_size("seq")
    members = lax.axis_size("rep")
    tok_rows, width = filter_taps.shape
    owners = members * devices
    rows = devices * SUB
    constants = [jnp.asarray(table) for table in tables(devices * tok_rows)]
    hbm = pl.BlockSpec(memory_space=pl.ANY)
    message = (owners, SUB, LANES)
    flat = (tok_rows, width)

    def buffers(shapes, dtype):
        return [pltpu.VMEM(shape, dtype) for shape in shapes]

    input_raw, filter_raw = pl.pallas_call(
        functools.partial(kernel, members, devices),
        out_shape=(
            jax.ShapeDtypeStruct(message, jnp.bfloat16),
            jax.ShapeDtypeStruct((members, devices, SUB, LANES), jnp.bfloat16),
        ),
        in_specs=[hbm] * 8,
        out_specs=(hbm, hbm),
        scratch_shapes=[pltpu.VMEM(table.shape, table.dtype) for table in constants]
        + buffers([(width * SUB, LANES)], jnp.float32)
        + buffers(
            [(2, *flat), flat, flat, out_proj.shape]
            + [message] * 3
            + [(devices, SUB, LANES), message]
            + [message, (devices, SUB, LANES), message, (devices, SUB, LANES)],
            jnp.bfloat16,
        )
        + buffers([(2 * rows, 3 * LANES)], jnp.float32)
        + buffers([(4, rows, 2 * LANES), (2 * rows, 3 * LANES)], jnp.bfloat16)
        + buffers([(5, rows, 2 * LANES)], jnp.float32)
        + [
            pltpu.SemaphoreType.DMA((KINDS,)),
            pltpu.SemaphoreType.DMA((KINDS,)),
            pltpu.SemaphoreType.DMA((8,)),
        ],
        compiler_params=pltpu.CompilerParams(
            collective_id=0, has_side_effects=True, vmem_limit_bytes=VMEM_LIMIT
        ),
        name="correlate",
    )(inputs.reshape(flat), cotangent.reshape(flat), filter_taps, out_proj, *constants)
    grad_input, grad_filter = pl.pallas_call(
        finish_kernel,
        out_shape=(jax.ShapeDtypeStruct(flat, jnp.bfloat16), jax.ShapeDtypeStruct(flat, jnp.float32)),
        in_specs=[hbm] * 2,
        out_specs=(hbm, hbm),
        scratch_shapes=buffers([message, (members, devices, SUB, LANES)], jnp.bfloat16)
        + buffers([(width * SUB, LANES)] * 2, jnp.float32)
        + buffers([flat], jnp.bfloat16)
        + buffers([flat], jnp.float32)
        + [pltpu.SemaphoreType.DMA((2,)), pltpu.SemaphoreType.DMA((2 * PARTS,))],
        compiler_params=pltpu.CompilerParams(vmem_limit_bytes=VMEM_LIMIT),
        name="finish",
    )(input_raw, filter_raw)
    return (grad_input.reshape(1, tok_rows, width), grad_filter)


def solution(mesh):
    return jax.shard_map(
        per_device,
        mesh=mesh,
        in_specs=(
            P("rep", "seq", "chan"),
            P("rep", "seq", "chan"),
            P("seq", "chan"),
            P("chan", None),
        ),
        out_specs=(P("rep", "seq", "chan"), P("seq", "chan")),
        check_vma=False,
    )
```

```python
import functools
import math

import jax
import jax.numpy as jnp
import numpy as np
from jax import lax
from jax.experimental import pallas as pl
from jax.experimental.pallas import tpu as pltpu
from jax.sharding import PartitionSpec as P

LANES = 128
SUB = 8
STEP = 128
WAVES = 2
PARTS = 2
VMEM_LIMIT = 60 * 1024 * 1024
MESH = pl.DeviceIdType.MESH
COT, SIG, TAP, GRAD, FILT, INP, SWAP = range(7)
KINDS = 7


def split_high_low(table):
    high = np.asarray(table, np.float32).astype(jnp.bfloat16)
    low = (table - high.astype(np.float64)).astype(np.float32).astype(jnp.bfloat16)
    return np.stack([high, low])


def tables(length):
    rows = length // LANES
    row_index = np.arange(rows)
    lane_index = np.arange(LANES)
    row_angle = ((4 * row_index[:, None] + 1) * row_index[None, :] % (4 * rows)) * (2.0 * math.pi / (4 * rows))
    twist_angle = ((4 * row_index[:, None] + 1) * lane_index[None, :] % (4 * length)) * (2.0 * math.pi / (4 * length))
    lane_angle = (lane_index[:, None] * lane_index[None, :] % LANES) * (2.0 * math.pi / LANES)
    row_forward = np.concatenate([np.cos(row_angle), -np.sin(row_angle)], axis=0)
    lane_cos, lane_sin = np.cos(lane_angle), np.sin(lane_angle)
    lane_forward = np.block([[lane_cos, -lane_sin], [lane_sin, lane_cos]])
    lane_inverse = np.block([[lane_cos, lane_sin], [-lane_sin, lane_cos]])
    forward_high, forward_low = split_high_low(row_forward)
    lane_tables = []
    for table in (lane_forward, lane_inverse):
        high, low = split_high_low(table)
        lane_tables.append(np.concatenate([high, high, low], axis=0))
    return (
        np.concatenate([forward_high, forward_low], axis=1),
        np.concatenate(list(split_high_low(row_forward.T / length)), axis=1),
        np.stack(lane_tables),
        np.stack([np.cos(twist_angle), np.sin(twist_angle)]).astype(np.float32),
    )


def dot(left, right):
    return jnp.dot(left, right, preferred_element_type=jnp.float32)


def transposed(block):
    at_row = lax.broadcasted_iota(jnp.int32, block.shape, 0)
    at_lane = lax.broadcasted_iota(jnp.int32, block.shape, 1)
    identity = jnp.where(at_row == at_lane, 1.0, 0.0).astype(jnp.bfloat16)
    return block.astype(jnp.float32).T


def store_split(ref, slot, at_rows, at_lanes, value):
    high = value.astype(jnp.bfloat16)
    ref[2 * slot, at_rows, at_lanes] = high
    ref[2 * slot + 1, at_rows, at_lanes] = (value - high.astype(jnp.float32)).astype(jnp.bfloat16)


def kernel(
    members, devices,
    signal_hbm, cot_hbm, taps_hbm, proj_hbm, forward_hbm, inverse_hbm, lane_hbm, twist_hbm,
    input_got, filter_all,
    forward, inverse, lane, twist, work, cots, signal_ref, taps_ref, proj_ref,
    signal_send, taps_send, grad_send, filter_send, input_send,
    signal_got, taps_got, grad_got, filter_got,
    outer, inner, pieces, untwisted, spectra, send_sem, recv_sem, load_sem,
):
    member = lax.axis_index("rep")
    place = lax.axis_index("seq")
    half = lax.axis_index("chan")
    owners = members * devices
    me = member * devices + place
    rows = devices * SUB
    width = signal_ref.shape[1]
    chunk = signal_ref.shape[0] // SUB

    other_member = 1 - member

    def device(at_member, at_place, part):
        return {"rep": at_member, "seq": at_place, "chan": part}

    def around(start, count, first, body):
        def step(at, carry):
            body(lax.rem(start + at, count))
            return carry

        lax.fori_loop(first, count, step, 0)

    barrier = pltpu.get_barrier_semaphore()

    def others(body):
        around(place, devices, 1, lambda at_place: body(member, at_place))
        around(place, devices, 0, lambda at_place: body(other_member, at_place))

    def others_of_member(body):
        around(place, devices, 1, body)

    def others_in_waves(body):
        turns = devices // WAVES
        turn = place // WAVES
        for wave in range(WAVES):
            around(turn, turns, 1, lambda at: body(member, at * WAVES + wave))

            @pl.when(lax.rem(place, WAVES) != wave)
            def _():
                body(member, turn * WAVES + wave)

            around(turn, turns, 0, lambda at: body(other_member, at * WAVES + wave))

    def greet(target):
        pl.semaphore_signal(barrier, inc=1, device_id=target, device_id_type=MESH)

    greet(device(member, place, 1 - half))
    others(lambda at_member, at_place: greet(device(at_member, at_place, half)))

    loads = [
        pltpu.make_async_copy(source, target_ref, load_sem.at[at])
        for at, (source, target_ref) in enumerate(
            (
                (taps_hbm, taps_ref),
                (signal_hbm, signal_ref),
                (cot_hbm, cots.at[half]),
                (proj_hbm, proj_ref),
                (forward_hbm, forward),
                (lane_hbm, lane),
                (twist_hbm, twist),
                (inverse_hbm, inverse),
            )
        )
    ]
    for copy in loads:
        copy.start()

    def spread(source, target_ref):
        for j in range(SUB):
            work[pl.ds(j, width, stride=SUB), :] = source(j)
        target_ref[...] = work[...].reshape(width, SUB, LANES).astype(jnp.bfloat16)

    def block_of(ref):
        return lambda j: transposed(ref[j * chunk : (j + 1) * chunk, :])

    loads[0].wait()
    spread(block_of(taps_ref), taps_send)
    loads[1].wait()
    spread(block_of(signal_ref), signal_send)
    loads[2].wait()
    pl.semaphore_wait(barrier, owners)

    def remote(kind, source, target_ref, target):
        return pltpu.make_async_remote_copy(
            src_ref=source, dst_ref=target_ref, send_sem=send_sem.at[kind], recv_sem=recv_sem.at[kind],
            device_id=target, device_id_type=MESH,
        )

    cot_copy = remote(COT, cots.at[half], cots.at[half], device(member, place, 1 - half))
    cot_copy.start()

    def exchange(kind, send_ref, got_ref, order=others):
        order(
            lambda at_member, at_place: remote(
                kind, send_ref.at[at_member * devices + at_place], got_ref.at[me], device(at_member, at_place, half)
            ).start()
        )
        pltpu.make_async_copy(send_ref.at[me], got_ref.at[me], recv_sem.at[kind]).start()

    def arrived(kind, got_ref):
        pltpu.make_async_copy(got_ref, got_ref, recv_sem.at[kind]).wait()

    def sent(kind, send_ref, count):
        part = send_ref.at[pl.ds(0, count)]
        pltpu.make_async_copy(part, part, send_sem.at[kind]).wait()

    others_of_member(
        lambda other: remote(
            TAP, taps_send.at[member * devices + other], taps_got.at[place], device(member, other, half)
        ).start()
    )
    pltpu.make_async_copy(taps_send.at[me], taps_got.at[place], recv_sem.at[TAP]).start()
    exchange(SIG, signal_send, signal_got)

    loads[3].wait()
    cot_copy.wait_recv()

    def mixed(j):
        total = None
        for part in range(2):
            term = lax.dot_general(
                proj_ref[:, part * width : (part + 1) * width],
                cots[part, j * chunk : (j + 1) * chunk, :],
                (((1,), (1,)), ((), ())),
                preferred_element_type=jnp.float32,
            )
            total = term if total is None else total + term
        return total

    spread(mixed, grad_send)
    exchange(GRAD, grad_send, grad_got, others_in_waves)

    for copy in loads[4:]:
        copy.wait()

    steps = [slice(at, at + STEP) for at in range(0, rows, STEP)]
    lower = [slice(rows + at, rows + at + STEP) for at in range(0, rows, STEP)]
    real_lanes, imag_lanes = slice(0, LANES), slice(LANES, 2 * LANES)

    def lane_dot(slot, table):
        high, low = pieces[2 * slot], pieces[2 * slot + 1]
        return dot(jnp.concatenate([high, low, high], axis=1), lane[table])

    def rows_forward(values):
        outer[:, : values.shape[1]] = dot(forward[...], jnp.concatenate([values, values], axis=0))

    def lanes_forward(first, which):
        for at in which:
            lanes = slice(at * LANES, (at + 1) * LANES)
            slot = at % 2
            for upper_rows, lower_rows in zip(steps, lower):
                real, imag = outer[upper_rows, lanes], outer[lower_rows, lanes]
                cosine, sine = twist[0, upper_rows], twist[1, upper_rows]
                store_split(pieces, slot, upper_rows, real_lanes, real * cosine + imag * sine)
                store_split(pieces, slot, upper_rows, imag_lanes, imag * cosine - real * sine)
            spectra[first + at] = lane_dot(slot, 0)

    def member_rows(ref, at):
        return ref[pl.ds(at * devices, devices)].reshape(rows, LANES)

    def gathered(ref):
        return jnp.concatenate([member_rows(ref, at) for at in (member, other_member)], axis=1)

    arrived(TAP, taps_got)
    arrived(SIG, signal_got)
    rows_forward(jnp.concatenate([gathered(signal_got), taps_got[...].reshape(rows, LANES)], axis=1))
    lanes_forward(0, (0, 1, 2))
    arrived(GRAD, grad_got)
    rows_forward(gathered(grad_got))
    lanes_forward(3, (0,))

    def conj_product(pairs, at_rows):
        real_total = imag_total = None
        for first, second in pairs:
            first_real, first_imag = spectra[first, at_rows, real_lanes], spectra[first, at_rows, imag_lanes]
            second_real, second_imag = spectra[second, at_rows, real_lanes], spectra[second, at_rows, imag_lanes]
            real = first_real * second_real + first_imag * second_imag
            imag = first_imag * second_real - first_real * second_imag
            real_total = real if real_total is None else real_total + real
            imag_total = imag if imag_total is None else imag_total + imag
        return real_total, imag_total

    def untransform(pairs, slot, lanes):
        for upper_rows in steps:
            real, imag = conj_product(pairs, upper_rows)
            pieces[2 * slot, upper_rows, real_lanes] = real.astype(jnp.bfloat16)
            pieces[2 * slot, upper_rows, imag_lanes] = imag.astype(jnp.bfloat16)
        high = pieces[2 * slot]
        inner[...] = dot(jnp.concatenate([high, high], axis=1), lane[1, 2 * LANES :])
        for upper_rows, lower_rows in zip(steps, lower):
            real, imag = inner[upper_rows, real_lanes], inner[upper_rows, imag_lanes]
            cosine, sine = twist[0, upper_rows], twist[1, upper_rows]
            untwisted[upper_rows, lanes] = (real * cosine - imag * sine).astype(jnp.bfloat16)
            untwisted[lower_rows, lanes] = (imag * cosine + real * sine).astype(jnp.bfloat16)

    def rows_inverse(lanes):
        values = untwisted[:, lanes]
        return dot(inverse[...], jnp.concatenate([values, values], axis=0)).astype(jnp.bfloat16)

    def input_result(turn):
        at = other_member if turn else member
        lanes = slice((1 + turn) * LANES, (2 + turn) * LANES)
        untransform(((3 + turn, 2),), 1, lanes)
        input_send[pl.ds(at * devices, devices)] = rows_inverse(lanes).reshape(devices, SUB, LANES)

        def send_input(at_place):
            remote(INP, input_send.at[at * devices + at_place], input_got.at[me], device(at, at_place, half)).start()

        around(place, devices, 0 if turn else 1, send_input)

    input_result(0)
    lanes_forward(3, (1,))
    untransform(((3, 0), (4, 1)), 0, slice(0, LANES))
    filter_send[...] = rows_inverse(slice(0, LANES)).reshape(devices, SUB, LANES)
    others_of_member(
        lambda other: remote(
            FILT, filter_send.at[other], filter_got.at[place], device(member, other, half)
        ).start()
    )
    pltpu.make_async_copy(filter_send.at[place], filter_got.at[place], recv_sem.at[FILT]).start()
    input_result(1)
    pltpu.make_async_copy(input_send.at[me], input_got.at[me], recv_sem.at[INP]).start()

    arrived(FILT, filter_got)
    swap = remote(SWAP, filter_got, filter_all.at[member], device(other_member, place, half))
    swap.start()
    keep = pltpu.make_async_copy(filter_got, filter_all.at[member], load_sem.at[0])
    keep.start()
    cot_copy.wait_send()
    sent(TAP, taps_send, devices - 1)
    sent(SIG, signal_send, owners - 1)
    sent(GRAD, grad_send, owners - 1)
    sent(FILT, filter_send, devices - 1)
    keep.wait()
    swap.wait()
    arrived(INP, input_got)
    sent(INP, input_send, owners - 1)


def finish_kernel(
    input_hbm, filter_hbm, input_out, filter_out,
    input_raw, filter_raw, input_work, filter_work, input_done, filter_done, load_sems, keep_sems,
):
    input_load = pltpu.make_async_copy(input_hbm, input_raw, load_sems.at[0])
    filter_load = pltpu.make_async_copy(filter_hbm, filter_raw, load_sems.at[1])
    filter_load.start()
    input_load.start()
    width = input_raw.shape[0]
    part_rows = input_out.shape[0] // PARTS
    keeps = []
    for load, raw, work, done, out in (
        (filter_load, filter_raw, filter_work, filter_done, filter_out),
        (input_load, input_raw, input_work, input_done, input_out),
    ):
        load.wait()
        work[...] = raw[...].astype(jnp.float32).reshape(work.shape)
        for j in range(SUB):
            block = work[pl.ds(j, width, stride=SUB), :]
            done[j * LANES : (j + 1) * LANES, :] = block.T.astype(done.dtype)
            if (j + 1) * LANES % part_rows == 0:
                part = pl.ds((j + 1) * LANES - part_rows, part_rows)
                keeps.append(pltpu.make_async_copy(done.at[part], out.at[part], keep_sems.at[len(keeps)]))
                keeps[-1].start()
    for keep in keeps:
        keep.wait()


def per_device(inputs, cotangent, filter_taps, out_proj):
    devices = lax.axis_size("seq")
    members = lax.axis_size("rep")
    tok_rows, width = filter_taps.shape
    owners = members * devices
    rows = devices * SUB
    constants = [jnp.asarray(table) for table in tables(devices * tok_rows)]
    hbm = pl.BlockSpec(memory_space=pl.ANY)
    message = (owners, SUB, LANES)
    flat = (tok_rows, width)

    def buffers(shapes, dtype):
        return [pltpu.VMEM(shape, dtype) for shape in shapes]

    input_raw, filter_raw = pl.pallas_call(
        functools.partial(kernel, members, devices),
        out_shape=(
            jax.ShapeDtypeStruct(message, jnp.bfloat16),
            jax.ShapeDtypeStruct((members, devices, SUB, LANES), jnp.bfloat16),
        ),
        in_specs=[hbm] * 8,
        out_specs=(hbm, hbm),
        scratch_shapes=[pltpu.VMEM(table.shape, table.dtype) for table in constants]
        + buffers([(width * SUB, LANES)], jnp.float32)
        + buffers(
            [(2, *flat), flat, flat, out_proj.shape]
            + [message] * 3
            + [(devices, SUB, LANES), message]
            + [message, (devices, SUB, LANES), message, (devices, SUB, LANES)],
            jnp.bfloat16,
        )
        + buffers([(2 * rows, 3 * LANES), (rows, 2 * LANES)], jnp.float32)
        + buffers([(4, rows, 2 * LANES), (2 * rows, 3 * LANES)], jnp.bfloat16)
        + buffers([(5, rows, 2 * LANES)], jnp.float32)
        + [
            pltpu.SemaphoreType.DMA((KINDS,)),
            pltpu.SemaphoreType.DMA((KINDS,)),
            pltpu.SemaphoreType.DMA((8,)),
        ],
        compiler_params=pltpu.CompilerParams(
            collective_id=0, has_side_effects=True, vmem_limit_bytes=VMEM_LIMIT
        ),
        name="correlate",
    )(inputs.reshape(flat), cotangent.reshape(flat), filter_taps, out_proj, *constants)
    grad_input, grad_filter = pl.pallas_call(
        finish_kernel,
        out_shape=(jax.ShapeDtypeStruct(flat, jnp.bfloat16), jax.ShapeDtypeStruct(flat, jnp.float32)),
        in_specs=[hbm] * 2,
        out_specs=(hbm, hbm),
        scratch_shapes=buffers([message, (members, devices, SUB, LANES)], jnp.bfloat16)
        + buffers([(width * SUB, LANES)] * 2, jnp.float32)
        + buffers([flat], jnp.bfloat16)
        + buffers([flat], jnp.float32)
        + [pltpu.SemaphoreType.DMA((2,)), pltpu.SemaphoreType.DMA((2 * PARTS,))],
        compiler_params=pltpu.CompilerParams(vmem_limit_bytes=VMEM_LIMIT),
        name="finish",
    )(input_raw, filter_raw)
    return (grad_input.reshape(1, tok_rows, width), grad_filter)


def solution(mesh):
    return jax.shard_map(
        per_device,
        mesh=mesh,
        in_specs=(
            P("rep", "seq", "chan"),
            P("rep", "seq", "chan"),
            P("seq", "chan"),
            P("chan", None),
        ),
        out_specs=(P("rep", "seq", "chan"), P("seq", "chan")),
        check_vma=False,
    )
```

```python
import functools
import math

import jax
import jax.numpy as jnp
import numpy as np
from jax import lax
from jax.experimental import pallas as pl
from jax.experimental.pallas import tpu as pltpu
from jax.sharding import PartitionSpec as P

LANES = 128
SUB = 8
STEP = 128
WAVES = 2
PARTS = 2
VMEM_LIMIT = 60 * 1024 * 1024
MESH = pl.DeviceIdType.MESH
COT, SIG, TAP, GRAD, FILT, INP, SWAP = range(7)
KINDS = 7


def split_high_low(table):
    high = np.asarray(table, np.float32).astype(jnp.bfloat16)
    low = (table - high.astype(np.float64)).astype(np.float32).astype(jnp.bfloat16)
    return np.stack([high, low])


def tables(length):
    rows = length // LANES
    row_index = np.arange(rows)
    lane_index = np.arange(LANES)
    row_angle = ((4 * row_index[:, None] + 1) * row_index[None, :] % (4 * rows)) * (2.0 * math.pi / (4 * rows))
    twist_angle = ((4 * row_index[:, None] + 1) * lane_index[None, :] % (4 * length)) * (2.0 * math.pi / (4 * length))
    lane_angle = (lane_index[:, None] * lane_index[None, :] % LANES) * (2.0 * math.pi / LANES)
    row_forward = np.concatenate([np.cos(row_angle), -np.sin(row_angle)], axis=0)
    lane_cos, lane_sin = np.cos(lane_angle), np.sin(lane_angle)
    lane_forward = np.block([[lane_cos, -lane_sin], [lane_sin, lane_cos]])
    lane_inverse = np.block([[lane_cos, lane_sin], [-lane_sin, lane_cos]])
    forward_high, forward_low = split_high_low(row_forward)
    lane_tables = []
    for table in (lane_forward, lane_inverse):
        high, low = split_high_low(table)
        lane_tables.append(np.concatenate([high, high, low], axis=0))
    return (
        np.concatenate([forward_high, forward_low], axis=1),
        np.concatenate(list(split_high_low(row_forward.T / length)), axis=1),
        np.stack(lane_tables),
        np.stack([np.cos(twist_angle), np.sin(twist_angle)]).astype(np.float32),
    )


def dot(left, right):
    return jnp.dot(left, right, preferred_element_type=jnp.float32)


def transposed(block):
    at_row = lax.broadcasted_iota(jnp.int32, block.shape, 0)
    at_lane = lax.broadcasted_iota(jnp.int32, block.shape, 1)
    identity = jnp.where(at_row == at_lane, 1.0, 0.0).astype(jnp.bfloat16)
    return block.astype(jnp.float32).T


def store_split(ref, slot, at_rows, at_lanes, value):
    high = value.astype(jnp.bfloat16)
    ref[2 * slot, at_rows, at_lanes] = high
    ref[2 * slot + 1, at_rows, at_lanes] = (value - high.astype(jnp.float32)).astype(jnp.bfloat16)


def kernel(
    members, devices,
    signal_hbm, cot_hbm, taps_hbm, proj_hbm, forward_hbm, inverse_hbm, lane_hbm, twist_hbm,
    input_got, filter_all,
    forward, inverse, lane, twist, work, cots, signal_ref, taps_ref, proj_ref,
    signal_send, taps_send, grad_send, filter_send, input_send,
    signal_got, taps_got, grad_got, filter_got,
    outer, pieces, untwisted, spectra, send_sem, recv_sem, load_sem,
):
    member = lax.axis_index("rep")
    place = lax.axis_index("seq")
    half = lax.axis_index("chan")
    owners = members * devices
    me = member * devices + place
    rows = devices * SUB
    width = signal_ref.shape[1]
    chunk = signal_ref.shape[0] // SUB

    other_member = 1 - member

    def device(at_member, at_place, part):
        return {"rep": at_member, "seq": at_place, "chan": part}

    def around(start, count, first, body):
        def step(at, carry):
            body(lax.rem(start + at, count))
            return carry

        lax.fori_loop(first, count, step, 0)

    barrier = pltpu.get_barrier_semaphore()

    def others(body):
        around(place, devices, 1, lambda at_place: body(member, at_place))
        around(place, devices, 0, lambda at_place: body(other_member, at_place))

    def others_of_member(body):
        around(place, devices, 1, body)

    def others_in_waves(body):
        turns = devices // WAVES
        turn = place // WAVES
        for wave in range(WAVES):
            around(turn, turns, 1, lambda at: body(member, at * WAVES + wave))

            @pl.when(lax.rem(place, WAVES) != wave)
            def _():
                body(member, turn * WAVES + wave)

            around(turn, turns, 0, lambda at: body(other_member, at * WAVES + wave))

    def greet(target):
        pl.semaphore_signal(barrier, inc=1, device_id=target, device_id_type=MESH)

    greet(device(member, place, 1 - half))
    others(lambda at_member, at_place: greet(device(at_member, at_place, half)))

    loads = [
        pltpu.make_async_copy(source, target_ref, load_sem.at[at])
        for at, (source, target_ref) in enumerate(
            (
                (taps_hbm, taps_ref),
                (signal_hbm, signal_ref),
                (cot_hbm, cots.at[half]),
                (proj_hbm, proj_ref),
                (forward_hbm, forward),
                (lane_hbm, lane),
                (twist_hbm, twist),
                (inverse_hbm, inverse),
            )
        )
    ]
    for copy in loads:
        copy.start()

    def spread(source, target_ref):
        for j in range(SUB):
            work[pl.ds(j, width, stride=SUB), :] = source(j)
        target_ref[...] = work[...].reshape(width, SUB, LANES).astype(jnp.bfloat16)

    def block_of(ref):
        return lambda j: transposed(ref[j * chunk : (j + 1) * chunk, :])

    loads[0].wait()
    spread(block_of(taps_ref), taps_send)
    loads[1].wait()
    spread(block_of(signal_ref), signal_send)
    loads[2].wait()
    pl.semaphore_wait(barrier, owners)

    def remote(kind, source, target_ref, target):
        return pltpu.make_async_remote_copy(
            src_ref=source, dst_ref=target_ref, send_sem=send_sem.at[kind], recv_sem=recv_sem.at[kind],
            device_id=target, device_id_type=MESH,
        )

    cot_copy = remote(COT, cots.at[half], cots.at[half], device(member, place, 1 - half))
    cot_copy.start()

    def exchange(kind, send_ref, got_ref, order=others):
        order(
            lambda at_member, at_place: remote(
                kind, send_ref.at[at_member * devices + at_place], got_ref.at[me], device(at_member, at_place, half)
            ).start()
        )
        pltpu.make_async_copy(send_ref.at[me], got_ref.at[me], recv_sem.at[kind]).start()

    def arrived(kind, got_ref):
        pltpu.make_async_copy(got_ref, got_ref, recv_sem.at[kind]).wait()

    def sent(kind, send_ref, count):
        part = send_ref.at[pl.ds(0, count)]
        pltpu.make_async_copy(part, part, send_sem.at[kind]).wait()

    others_of_member(
        lambda other: remote(
            TAP, taps_send.at[member * devices + other], taps_got.at[place], device(member, other, half)
        ).start()
    )
    pltpu.make_async_copy(taps_send.at[me], taps_got.at[place], recv_sem.at[TAP]).start()
    exchange(SIG, signal_send, signal_got)

    loads[3].wait()
    cot_copy.wait_recv()

    def mixed(j):
        total = None
        for part in range(2):
            term = lax.dot_general(
                proj_ref[:, part * width : (part + 1) * width],
                cots[part, j * chunk : (j + 1) * chunk, :],
                (((1,), (1,)), ((), ())),
                preferred_element_type=jnp.float32,
            )
            total = term if total is None else total + term
        return total

    spread(mixed, grad_send)
    exchange(GRAD, grad_send, grad_got, others_in_waves)

    for copy in loads[4:]:
        copy.wait()

    steps = [slice(at, at + STEP) for at in range(0, rows, STEP)]
    lower = [slice(rows + at, rows + at + STEP) for at in range(0, rows, STEP)]
    real_lanes, imag_lanes = slice(0, LANES), slice(LANES, 2 * LANES)

    def lane_dot(slot, table):
        high, low = pieces[2 * slot], pieces[2 * slot + 1]
        return dot(jnp.concatenate([high, low, high], axis=1), lane[table])

    def transform(values, first):
        count = values.shape[1] // LANES
        outer[:, : count * LANES] = dot(forward[...], jnp.concatenate([values, values], axis=0))
        for at in range(count):
            lanes = slice(at * LANES, (at + 1) * LANES)
            slot = at % 2
            for upper_rows, lower_rows in zip(steps, lower):
                real, imag = outer[upper_rows, lanes], outer[lower_rows, lanes]
                cosine, sine = twist[0, upper_rows], twist[1, upper_rows]
                store_split(pieces, slot, upper_rows, real_lanes, real * cosine + imag * sine)
                store_split(pieces, slot, upper_rows, imag_lanes, imag * cosine - real * sine)
            spectra[first + at] = lane_dot(slot, 0)

    def member_rows(ref, at):
        return ref[at * devices : (at + 1) * devices].reshape(rows, LANES)

    def gathered(ref):
        return jnp.concatenate([member_rows(ref, at) for at in range(members)], axis=1)

    arrived(TAP, taps_got)
    arrived(SIG, signal_got)
    transform(jnp.concatenate([gathered(signal_got), taps_got[...].reshape(rows, LANES)], axis=1), 0)
    arrived(GRAD, grad_got)
    transform(gathered(grad_got), 3)

    def conj_product(pairs, at_rows):
        real_total = imag_total = None
        for first, second in pairs:
            first_real, first_imag = spectra[first, at_rows, real_lanes], spectra[first, at_rows, imag_lanes]
            second_real, second_imag = spectra[second, at_rows, real_lanes], spectra[second, at_rows, imag_lanes]
            real = first_real * second_real + first_imag * second_imag
            imag = first_imag * second_real - first_real * second_imag
            real_total = real if real_total is None else real_total + real
            imag_total = imag if imag_total is None else imag_total + imag
        return real_total, imag_total

    def untransform(pairs, slot, lanes):
        for upper_rows in steps:
            real, imag = conj_product(pairs, upper_rows)
            pieces[2 * slot, upper_rows, real_lanes] = real.astype(jnp.bfloat16)
            pieces[2 * slot, upper_rows, imag_lanes] = imag.astype(jnp.bfloat16)
        high = pieces[2 * slot]
        outer[:rows, : 2 * LANES] = dot(jnp.concatenate([high, high], axis=1), lane[1, 2 * LANES :])
        for upper_rows, lower_rows in zip(steps, lower):
            real, imag = outer[upper_rows, real_lanes], outer[upper_rows, imag_lanes]
            cosine, sine = twist[0, upper_rows], twist[1, upper_rows]
            untwisted[upper_rows, lanes] = (real * cosine - imag * sine).astype(jnp.bfloat16)
            untwisted[lower_rows, lanes] = (imag * cosine + real * sine).astype(jnp.bfloat16)

    def rows_inverse(lanes):
        values = untwisted[:, lanes]
        return dot(inverse[...], jnp.concatenate([values, values], axis=0)).astype(jnp.bfloat16)

    untransform(((3, 0), (4, 1)), 0, slice(0, LANES))
    filter_send[...] = rows_inverse(slice(0, LANES)).reshape(devices, SUB, LANES)
    others_of_member(
        lambda other: remote(
            FILT, filter_send.at[other], filter_got.at[place], device(member, other, half)
        ).start()
    )
    pltpu.make_async_copy(filter_send.at[place], filter_got.at[place], recv_sem.at[FILT]).start()

    for turn in range(members):
        at = member if turn else other_member
        lanes = slice((1 + turn) * LANES, (2 + turn) * LANES)
        untransform(((3 + at, 2),), 1 - turn, lanes)
        input_send[pl.ds(at * devices, devices)] = rows_inverse(lanes).reshape(devices, SUB, LANES)

        def send_input(at_place, at=at):
            remote(INP, input_send.at[at * devices + at_place], input_got.at[me], device(at, at_place, half)).start()

        around(place, devices, 1 if turn else 0, send_input)
    pltpu.make_async_copy(input_send.at[me], input_got.at[me], recv_sem.at[INP]).start()

    arrived(FILT, filter_got)
    swap = remote(SWAP, filter_got, filter_all.at[member], device(other_member, place, half))
    swap.start()
    keep = pltpu.make_async_copy(filter_got, filter_all.at[member], load_sem.at[0])
    keep.start()
    cot_copy.wait_send()
    sent(TAP, taps_send, devices - 1)
    sent(SIG, signal_send, owners - 1)
    sent(GRAD, grad_send, owners - 1)
    sent(FILT, filter_send, devices - 1)
    keep.wait()
    swap.wait()
    arrived(INP, input_got)
    sent(INP, input_send, owners - 1)


def finish_kernel(
    input_hbm, filter_hbm, input_out, filter_out,
    input_raw, filter_raw, input_work, filter_work, input_done, filter_done, load_sems, keep_sems,
):
    input_load = pltpu.make_async_copy(input_hbm, input_raw, load_sems.at[0])
    filter_load = pltpu.make_async_copy(filter_hbm, filter_raw, load_sems.at[1])
    filter_load.start()
    input_load.start()
    width = input_raw.shape[0]
    part_rows = input_out.shape[0] // PARTS
    keeps = []
    for load, raw, work, done, out in (
        (filter_load, filter_raw, filter_work, filter_done, filter_out),
        (input_load, input_raw, input_work, input_done, input_out),
    ):
        load.wait()
        work[...] = raw[...].astype(jnp.float32).reshape(work.shape)
        for j in range(SUB):
            block = work[pl.ds(j, width, stride=SUB), :]
            done[j * LANES : (j + 1) * LANES, :] = block.T.astype(done.dtype)
            if (j + 1) * LANES % part_rows == 0:
                part = pl.ds((j + 1) * LANES - part_rows, part_rows)
                keeps.append(pltpu.make_async_copy(done.at[part], out.at[part], keep_sems.at[len(keeps)]))
                keeps[-1].start()
    for keep in keeps:
        keep.wait()


def per_device(inputs, cotangent, filter_taps, out_proj):
    devices = lax.axis_size("seq")
    members = lax.axis_size("rep")
    tok_rows, width = filter_taps.shape
    owners = members * devices
    rows = devices * SUB
    constants = [jnp.asarray(table) for table in tables(devices * tok_rows)]
    hbm = pl.BlockSpec(memory_space=pl.ANY)
    message = (owners, SUB, LANES)
    flat = (tok_rows, width)

    def buffers(shapes, dtype):
        return [pltpu.VMEM(shape, dtype) for shape in shapes]

    input_raw, filter_raw = pl.pallas_call(
        functools.partial(kernel, members, devices),
        out_shape=(
            jax.ShapeDtypeStruct(message, jnp.bfloat16),
            jax.ShapeDtypeStruct((members, devices, SUB, LANES), jnp.bfloat16),
        ),
        in_specs=[hbm] * 8,
        out_specs=(hbm, hbm),
        scratch_shapes=[pltpu.VMEM(table.shape, table.dtype) for table in constants]
        + buffers([(width * SUB, LANES)], jnp.float32)
        + buffers(
            [(2, *flat), flat, flat, out_proj.shape]
            + [message] * 3
            + [(devices, SUB, LANES), message]
            + [message, (devices, SUB, LANES), message, (devices, SUB, LANES)],
            jnp.bfloat16,
        )
        + buffers([(2 * rows, 3 * LANES)], jnp.float32)
        + buffers([(4, rows, 2 * LANES), (2 * rows, 3 * LANES)], jnp.bfloat16)
        + buffers([(5, rows, 2 * LANES)], jnp.float32)
        + [
            pltpu.SemaphoreType.DMA((KINDS,)),
            pltpu.SemaphoreType.DMA((KINDS,)),
            pltpu.SemaphoreType.DMA((8,)),
        ],
        compiler_params=pltpu.CompilerParams(
            collective_id=0, has_side_effects=True, vmem_limit_bytes=VMEM_LIMIT
        ),
        name="correlate",
    )(inputs.reshape(flat), cotangent.reshape(flat), filter_taps, out_proj, *constants)
    grad_input, grad_filter = pl.pallas_call(
        finish_kernel,
        out_shape=(jax.ShapeDtypeStruct(flat, jnp.bfloat16), jax.ShapeDtypeStruct(flat, jnp.float32)),
        in_specs=[hbm] * 2,
        out_specs=(hbm, hbm),
        scratch_shapes=buffers([message, (members, devices, SUB, LANES)], jnp.bfloat16)
        + buffers([(width * SUB, LANES)] * 2, jnp.float32)
        + buffers([flat], jnp.bfloat16)
        + buffers([flat], jnp.float32)
        + [pltpu.SemaphoreType.DMA((2,)), pltpu.SemaphoreType.DMA((2 * PARTS,))],
        compiler_params=pltpu.CompilerParams(vmem_limit_bytes=VMEM_LIMIT),
        name="finish",
    )(input_raw, filter_raw)
    return (grad_input.reshape(1, tok_rows, width), grad_filter)


def solution(mesh):
    return jax.shard_map(
        per_device,
        mesh=mesh,
        in_specs=(
            P("rep", "seq", "chan"),
            P("rep", "seq", "chan"),
            P("seq", "chan"),
            P("chan", None),
        ),
        out_specs=(P("rep", "seq", "chan"), P("seq", "chan")),
        check_vma=False,
    )
```
